32 devices in a mesh: gx: 4 (over y, x), gy: 4 (over z), band: 2 (over core).
Axes of the slice: x: 2, y: 2, z: 4, core: 2. Of those that a mesh axis runs over, the one named last changes fastest.
Arguments:
- orbitals: float32 [32, 32, 32, 128], P('band', 'gx', 'gy'), may hold values from -6 to 6
- local_potential: float32 [32, 32, 128], P('gx', 'gy'), may hold values from -4 to 0
- atom_cell: int32 [4, 4, 2], P('gx', 'gy'), may hold values from 0 to 8191
- support_offset: int32 [3, 4, 4, 2, 512], P(None, 'gx', 'gy'), may hold values from -6 to 6
- projector: float32 [4, 4, 2, 4, 512], P('gx', 'gy'), may hold values from -0.5 to 0.5
- coupling: float32 [4, 4, 2, 4], P('gx', 'gy'), may hold values from 8 to 32
Outputs:
- orbitals_new: float32 [32, 32, 32, 128], P('band', 'gx', 'gy')
- residual: float32 [32, 32, 32, 128], P('band', 'gx', 'gy')
- subspace: float32 [32, 32], replicated
The draws below stay inside these ranges and needn't reach their ends.
Inputs may be any that keep to these rules, and one draw needn't show every extreme that they name: Each domain owns exactly 2 atoms; atom_cell is x * 8 * 128 + y * 128 + z for the atom's cell (x, y, z) counted within its domain. `support_offset`: support points of one atom may repeat; they may lie in neighbouring domains or outside the grid.
All inputs are finite; a program needn't handle non-finite values.
Results may differ from the reference program's by a relative error of at most 0.0003.
Values sent between devices are 32-bit elements; how exact they have to be, the bound alone decides.
A program may use at most 64 MiB of HBM per device.

```python
import math
import jax
import jax.numpy as jnp
from jax import lax

ORBS = 32
NPROJ = 4
SUP = 512
REACH = 6
CX = 8
CY = 8
CZ = 128
ATOMS_DEV = 2
DOM_X = 4
DOM_Y = 4
NX = 32
NY = 32
NZ = 128
NCELLS = 131072


def with_ends(values, rng, smallest, largest):
    longest = values.shape.index(max(values.shape))
    spots = []
    for shift in (0, 1):
        where = [jax.random.randint(jax.random.fold_in(rng, axis), (), 0, length) for axis, length in enumerate(values.shape)]
        where[longest] = (where[longest] + shift) % values.shape[longest]
        spots.append(tuple(where))
    return values.at[spots[0]].set(smallest).at[spots[1]].set(largest)


def shard_levels(key, extent, cuts, least, largest):
    gain, own = 1.0, jax.random.fold_in(key, 6)
    for axis_at, parts in cuts:
        draws = jnp.exp(jax.random.uniform(jax.random.fold_in(own, axis_at), (parts,), jnp.float32, least / len(cuts), largest / len(cuts)))
        gain = gain * jnp.repeat(draws, extent[axis_at] // parts).reshape([-1 if axis == axis_at else 1 for axis in range(len(extent))])
    return gain


def noise(stream_key, shape, deviation, reach, pieces=(), held_as=jnp.bfloat16):
    entries = deviation * jax.random.normal(stream_key, shape, jnp.float32)
    if pieces:
        entries = entries * shard_levels(stream_key, shape, pieces, -0.22, 0.18)
    return jnp.clip(entries, -reach, reach).astype(held_as)


def setup_inputs(seed: int = 0) -> dict:
    key_list = jax.random.split(jax.random.key(seed), 7)
    orbitals = noise(key_list[0], (ORBS, NX, NY, NZ), 1.0, 6.0, ((0, 2), (1, 4), (2, 4)), jnp.float32)
    local_potential = jnp.clip(-4.0 + 4.0 * jax.random.uniform(key_list[1], (NX, NY, NZ), jnp.float32) ** shard_levels(key_list[1], (NX, NY, NZ), ((0, 4), (1, 4)), -0.2, 0.2), -4.0, 0.0)
    atom_cell = with_ends(jax.random.randint(key_list[2], (DOM_X, DOM_Y, ATOMS_DEV), 0, CX * CY * CZ), jax.random.fold_in(key_list[2], 1), 0, (CX * CY * CZ) - 1).astype(jnp.int32)
    support_offset = with_ends(jax.random.randint(key_list[3], (3, DOM_X, DOM_Y, ATOMS_DEV, SUP), -REACH, REACH + 1), jax.random.fold_in(key_list[3], 1), -REACH, REACH).astype(jnp.int32)
    projector = noise(key_list[4], (DOM_X, DOM_Y, ATOMS_DEV, NPROJ, SUP), (SUP // 4) ** -0.5, 0.5, ((0, 4), (1, 4)), jnp.float32)
    coupling = jnp.clip(jnp.exp(math.log(32.0) - 1.3862944 * jax.random.uniform(key_list[5], (DOM_X, DOM_Y, ATOMS_DEV, NPROJ), jnp.float32) ** shard_levels(key_list[5], (DOM_X, DOM_Y, ATOMS_DEV, NPROJ), ((0, 4), (1, 4)), -0.2, 0.2)), 8.0, 32.0)
    return dict(orbitals=orbitals, local_potential=local_potential, atom_cell=atom_cell, support_offset=support_offset, projector=projector, coupling=coupling)


spacing = 0.4
low_edge = 6.0
top_edge = 150.0
stencil = (-5369.0 / 1800.0, 12.0 / 7.0, -15.0 / 56.0, 10.0 / 189.0, -1.0 / 112.0, 2.0 / 1925.0, -1.0 / 16632.0)

def laplace_term(field_one):
    padded = jnp.pad(field_one, 6)
    size_x, size_y, size_z = field_one.shape
    summed = 3.0 * stencil[0] * field_one
    for stride in range(1, 7):
        along_x = padded[6 + stride:6 + stride + size_x, 6:6 + size_y, 6:6 + size_z] + padded[6 - stride:6 - stride + size_x, 6:6 + size_y, 6:6 + size_z]
        along_y = padded[6:6 + size_x, 6 + stride:6 + stride + size_y, 6:6 + size_z] + padded[6:6 + size_x, 6 - stride:6 - stride + size_y, 6:6 + size_z]
        along_z = padded[6:6 + size_x, 6:6 + size_y, 6 + stride:6 + stride + size_z] + padded[6:6 + size_x, 6:6 + size_y, 6 - stride:6 - stride + size_z]
        summed = summed + stencil[stride] * (along_x + along_y + along_z)
    return -0.5 / spacing ** 2 * summed

def support_cells(atom_cell, support_offset):
    domain_x = lax.broadcasted_iota(jnp.int32, atom_cell.shape, 0)
    domain_y = lax.broadcasted_iota(jnp.int32, atom_cell.shape, 1)
    home_x = domain_x * CX + atom_cell // (CY * CZ)
    home_y = domain_y * CY + atom_cell // CZ % CY
    home_z = atom_cell % CZ
    coord_x = home_x[..., None] + support_offset[0]
    coord_y = home_y[..., None] + support_offset[1]
    coord_z = home_z[..., None] + support_offset[2]
    inside = (coord_x >= 0) & (coord_x < NX) & (coord_y >= 0) & (coord_y < NY) & (coord_z >= 0) & (coord_z < NZ)
    cell_index = (jnp.clip(coord_x, 0, NX - 1) * NY + jnp.clip(coord_y, 0, NY - 1)) * NZ + jnp.clip(coord_z, 0, NZ - 1)
    return (cell_index.astype(jnp.int32), inside.astype(jnp.float32))

def apply_one(field_one, local_potential, cell_index, inside, projector, coupling):
    flat_field = field_one.reshape(-1)
    sampled = flat_field[cell_index] * inside
    coefficients = jnp.einsum('xyanS,xyaS->xyan', projector, sampled, precision=lax.Precision.HIGHEST)
    spread = jnp.einsum('xyanS,xyan->xyaS', projector, coupling * coefficients, precision=lax.Precision.HIGHEST) * inside
    projector_term = jnp.zeros_like(flat_field).at[cell_index.reshape(-1)].add(spread.reshape(-1))
    return laplace_term(field_one) + local_potential * field_one + projector_term.reshape(field_one.shape)

def reference(orbitals, local_potential, atom_cell, support_offset, projector, coupling):
    cell_index, inside = support_cells(atom_cell, support_offset)

    def apply_block(orbital_block):

        def single(field_one):
            return apply_one(field_one, local_potential, cell_index, inside, projector, coupling)
        return lax.map(single, orbital_block)
    middle = 0.5 * (top_edge + low_edge)
    half_width = 0.5 * (top_edge - low_edge)
    first_term = (apply_block(orbitals) - middle * orbitals) / half_width
    filtered = 2.0 * (apply_block(first_term) - middle * first_term) / half_width - orbitals
    flat_filtered = filtered.reshape(ORBS, -1)
    intersection = jnp.einsum('kc,lc->kl', flat_filtered, flat_filtered, precision=lax.Precision.HIGHEST) / NCELLS
    factor = jnp.linalg.cholesky(intersection)
    identity = jnp.eye(ORBS, dtype=jnp.float32)
    inverse = lax.linalg.triangular_solve(factor, identity, left_side=True, lower=True)
    rotated = jnp.dot(inverse, flat_filtered, precision=lax.Precision.HIGHEST)
    image_all = apply_block(rotated.reshape(orbitals.shape)).reshape(ORBS, -1)
    subspace = jnp.einsum('kc,lc->kl', rotated, image_all, precision=lax.Precision.HIGHEST) / NCELLS
    residual = (image_all - jnp.einsum('kl,kc->lc', subspace, rotated, precision=lax.Precision.HIGHEST)) / half_width
    return (rotated.reshape(orbitals.shape), residual.reshape(orbitals.shape), subspace)
```

```python
import functools

import jax
import jax.numpy as jnp
import numpy as np
from jax import lax
from jax.experimental import pallas as pl
from jax.experimental.pallas import tpu as pltpu
from jax.sharding import PartitionSpec as P

spacing = 0.4
low_edge = 6.0
top_edge = 150.0
stencil = (
    -5369.0 / 1800.0,
    12.0 / 7.0,
    -15.0 / 56.0,
    10.0 / 189.0,
    -1.0 / 112.0,
    2.0 / 1925.0,
    -1.0 / 16632.0,
)
highest = lax.Precision.HIGHEST


def with_halo(cells, sides, width):
    for axis, dim in sides:
        count = lax.axis_size(axis)
        ends = count - 1
        head = lax.slice_in_dim(cells, 0, width, axis=dim)
        tail = lax.slice_in_dim(cells, cells.shape[dim] - width, cells.shape[dim], axis=dim)
        cells = jnp.concatenate(
            [
                lax.ppermute(tail, axis, [(i, (i + 1) % count) for i in range(ends)]),
                cells,
                lax.ppermute(head, axis, [((i + 1) % count, i) for i in range(ends)]),
            ],
            axis=dim,
        )
    return cells


def kinetic_part(extended, orbital_block):
    size_x, size_y, size_z = (
        orbital_block.shape[1],
        orbital_block.shape[2],
        orbital_block.shape[3],
    )
    padded_z = jnp.pad(orbital_block, ((0, 0), (0, 0), (0, 0), (6, 6)))
    summed = 3.0 * stencil[0] * orbital_block
    for stride in range(1, 7):
        along_x = (
            extended[:, 6 + stride : 6 + stride + size_x, 6 : 6 + size_y]
            + extended[:, 6 - stride : 6 - stride + size_x, 6 : 6 + size_y]
        )
        along_y = (
            extended[:, 6 : 6 + size_x, 6 + stride : 6 + stride + size_y]
            + extended[:, 6 : 6 + size_x, 6 - stride : 6 - stride + size_y]
        )
        along_z = (
            padded_z[..., 6 + stride : 6 + stride + size_z]
            + padded_z[..., 6 - stride : 6 - stride + size_z]
        )
        summed = summed + stencil[stride] * (along_x + along_y + along_z)
    return -0.5 / spacing**2 * summed


def prepare_tables(atom_cell, support_offset, projector, size_x, size_y, size_z):
    home_cell = atom_cell[..., None]
    relative = jnp.stack(
        [
            home_cell // (size_y * size_z) + support_offset[0],
            home_cell // size_z % size_y + support_offset[1],
            home_cell % size_z + support_offset[2],
        ]
    )
    rel_near = with_halo(relative, (("gx", 1), ("gy", 2)), 1)
    beta_near = with_halo(projector, (("gx", 0), ("gy", 1)), 1)
    atom_count, proj_count = (projector.shape[2], projector.shape[3])
    cell_count = size_x * size_y * size_z
    frame_x = (lax.broadcasted_iota(jnp.int32, (3, 3, 1, 1), 0) - 1) * size_x
    frame_y = (lax.broadcasted_iota(jnp.int32, (3, 3, 1, 1), 1) - 1) * size_y
    coord_x = rel_near[0] + frame_x
    coord_y = rel_near[1] + frame_y
    coord_z = rel_near[2]
    inside = (
        (coord_x >= 0)
        & (coord_x < size_x)
        & (coord_y >= 0)
        & (coord_y < size_y)
        & (coord_z >= 0)
        & (coord_z < size_z)
    ).astype(jnp.float32)
    cell_index = (
        jnp.clip(coord_x, 0, size_x - 1) * size_y + jnp.clip(coord_y, 0, size_y - 1)
    ) * size_z + jnp.clip(coord_z, 0, size_z - 1)
    near_columns = jnp.arange(9 * atom_count * proj_count, dtype=jnp.int32).reshape(
        3, 3, atom_count, proj_count, 1
    )
    near_flat = near_columns * cell_count + cell_index[:, :, :, None, :]
    near_values = beta_near * inside[:, :, :, None, :]
    table_near = (
        jnp.zeros((9 * atom_count * proj_count * cell_count,), jnp.float32)
        .at[near_flat.reshape(-1)]
        .add(near_values.reshape(-1))
    )
    table_near = table_near.reshape(3, 3, atom_count, proj_count, cell_count)
    own_rel = relative[:, 0, 0]
    own_x = own_rel[0] + 6
    own_y = own_rel[1] + 6
    own_z = own_rel[2]
    own_zin = ((own_z >= 0) & (own_z < size_z)).astype(jnp.float32)
    own_index = (own_x * (size_y + 12) + own_y) * size_z + jnp.clip(own_z, 0, size_z - 1)
    ext_count = (size_x + 12) * (size_y + 12) * size_z
    own_columns = jnp.arange(atom_count * proj_count, dtype=jnp.int32).reshape(
        atom_count, proj_count, 1
    )
    own_flat = own_columns * ext_count + own_index[:, None, :]
    own_values = projector[0, 0] * own_zin[:, None, :]
    table_own = (
        jnp.zeros((atom_count * proj_count * ext_count,), jnp.float32)
        .at[own_flat.reshape(-1)]
        .add(own_values.reshape(-1))
    )
    table_own = table_own.reshape(atom_count, proj_count, ext_count)
    return (table_near, table_own)


def apply_hamiltonian(orbital_block, local_potential, tables, coupling_own):
    table_near, table_own = tables
    orb_count = orbital_block.shape[0]
    atom_count, proj_count = coupling_own.shape
    flat_block = orbital_block.reshape(orb_count, -1)
    extended = with_halo(orbital_block, (("gx", 1), ("gy", 2)), 6)
    kinetic = kinetic_part(extended, orbital_block)
    partial_terms = jnp.einsum("ijanc,bc->ijanb", table_near, flat_block, precision=highest)
    received = with_halo(partial_terms.reshape(1, 1, -1), (("gx", 0), ("gy", 1)), 1)
    grouped = received.reshape(3, 3, 3, 3, atom_count, proj_count, orb_count)
    coefficients = grouped[1, 1, 1, 1]
    for row_pos in range(3):
        for col_pos in range(3):
            if row_pos != 1 or col_pos != 1:
                coefficients = coefficients + grouped[row_pos, col_pos, 2 - row_pos, 2 - col_pos]
    scaled = coupling_own[:, :, None] * coefficients
    near_coefs = with_halo(scaled.reshape(1, 1, -1), (("gx", 0), ("gy", 1)), 1)
    near_coefs = near_coefs.reshape(3, 3, atom_count, proj_count, orb_count)
    projector_term = jnp.einsum("ijanc,ijanb->bc", table_near, near_coefs, precision=highest)
    return kinetic + local_potential * orbital_block + projector_term.reshape(orbital_block.shape)


def inverse_factor(intersection):
    factor = jnp.linalg.cholesky(intersection)
    identity = jnp.eye(intersection.shape[0], dtype=jnp.float32)
    return lax.linalg.triangular_solve(factor, identity, left_side=True, lower=True)


def per_device_halo(orbitals, local_potential, atom_cell, support_offset, projector, coupling):
    orb_count, size_x, size_y, size_z = orbitals.shape
    tables = prepare_tables(atom_cell, support_offset, projector, size_x, size_y, size_z)
    coupling_own = coupling[0, 0]

    def hamiltonian(orbital_block):
        return apply_hamiltonian(orbital_block, local_potential, tables, coupling_own)

    middle = 0.5 * (top_edge + low_edge)
    half_width = 0.5 * (top_edge - low_edge)
    total_cells = float(size_x * size_y * size_z * lax.axis_size("gx") * lax.axis_size("gy"))
    band_start = lax.axis_index("band") * orb_count
    first_term = (hamiltonian(orbitals) - middle * orbitals) / half_width
    filtered = 2.0 * (hamiltonian(first_term) - middle * first_term) / half_width - orbitals
    filt_flat = filtered.reshape(orb_count, -1)
    orbs_all = orb_count * lax.axis_size("band")
    empty_square = jnp.zeros((orbs_all, orbs_all), jnp.float32)
    whole_block = lax.all_gather(filt_flat, "band", axis=0, tiled=True)
    over_cols = jnp.einsum("kc,lc->kl", whole_block, filt_flat, precision=highest) / total_cells
    intersection = lax.psum(
        lax.dynamic_update_slice(empty_square, over_cols, (0, band_start)), ("gx", "gy", "band")
    )
    inverse = inverse_factor(intersection)
    rotated_all = jnp.dot(inverse, whole_block, precision=highest)
    rotated = lax.dynamic_slice_in_dim(rotated_all, band_start, orb_count, 0)
    image_own = hamiltonian(rotated.reshape(orbitals.shape)).reshape(orb_count, -1)
    sub_cols = jnp.einsum("kc,lc->kl", rotated_all, image_own, precision=highest) / total_cells
    subspace = lax.psum(
        lax.dynamic_update_slice(empty_square, sub_cols, (0, band_start)), ("gx", "gy", "band")
    )
    cols_own = lax.dynamic_slice_in_dim(subspace, band_start, orb_count, 1)
    residual = (
        image_own - jnp.einsum("kl,kc->lc", cols_own, rotated_all, precision=highest)
    ) / half_width
    return (rotated.reshape(orbitals.shape), residual.reshape(orbitals.shape), subspace)


MESH = pl.DeviceIdType.MESH
reach = 6
box = 2 * reach + 1
box_y = 16
pad_y = 8
scale = -0.5 / spacing**2


def gather_kernel(dims, orb_ref, pot_ref, pack_ref, orb_out, pot_out, pack_out, local_sem, send_sem, recv_sem):
    dom_x, dom_y = dims
    count = dom_x * dom_y
    my_x, my_y = lax.axis_index("gx"), lax.axis_index("gy")
    me = my_x * dom_y + my_y

    barrier = pltpu.get_barrier_semaphore()

    def greet(step, carry):
        peer = lax.rem(me + step, count)
        pl.semaphore_signal(
            barrier, inc=1, device_id={"gx": peer // dom_y, "gy": lax.rem(peer, dom_y)}, device_id_type=MESH
        )
        return carry

    def parts(peer, source_x, source_y):
        source = source_x * dom_y + source_y
        target = {"gx": peer // dom_y, "gy": lax.rem(peer, dom_y)}
        pairs = (
            (pack_ref, pack_out.at[source]),
            (pot_ref, pot_out.at[source_x, :, source_y]),
            (orb_ref.at[peer], orb_out.at[source_x, :, source_y]),
        )
        return [
            pltpu.make_async_remote_copy(
                src_ref=src,
                dst_ref=dst,
                send_sem=send_sem.at[kind, peer],
                recv_sem=recv_sem.at[kind, source],
                device_id=target,
                device_id_type=MESH,
            )
            for kind, (src, dst) in enumerate(pairs)
        ]

    lax.fori_loop(1, count, greet, 0)
    own = [
        pltpu.make_async_copy(pack_ref, pack_out.at[me], local_sem.at[0]),
        pltpu.make_async_copy(pot_ref, pot_out.at[my_x, :, my_y], local_sem.at[1]),
        pltpu.make_async_copy(orb_ref.at[me], orb_out.at[my_x, :, my_y], local_sem.at[2]),
    ]
    for copy in own:
        copy.start()
    pl.semaphore_wait(barrier, count - 1)

    def send(step, carry):
        for copy in parts(lax.rem(me + step, count), my_x, my_y):
            copy.start()
        return carry

    def finish(step, carry):
        peer = lax.rem(me + step, count)
        for copy in parts(peer, my_x, my_y):
            copy.wait_send()
        for copy in parts(peer, peer // dom_y, lax.rem(peer, dom_y)):
            copy.wait_recv()
        return carry

    lax.fori_loop(1, count, send, 0)
    lax.fori_loop(1, count, finish, 0)
    for copy in own:
        copy.wait()


def compute_kernel(
    dims, home_ref, orb_ref, pot_ref, pack_ref, coup_ref, along_ref, filt_out, image_out, table, field, out, sums, coefs
):
    count, atom_count, proj_count = dims
    nx, ny, nz = orb_ref.shape
    points = pack_ref.shape[2]
    rows = box * box_y
    wide = 16
    lane = lax.broadcasted_iota(jnp.int32, (rows, nz), 1)
    row_xy = lax.broadcasted_iota(jnp.int32, (rows, points), 0)
    row_z = lax.broadcasted_iota(jnp.int32, (wide, points), 0)

    def build(dom, carry):
        for atom in range(atom_count):
            cell = pack_ref[dom, 8 + atom : 9 + atom, :].astype(jnp.int32)
            hot_xy = jnp.where(row_xy == lax.shift_right_arithmetic(cell, 4), 1.0, 0.0).astype(jnp.bfloat16)
            hot_z = row_z == (cell & 15)
            values = jnp.concatenate(
                [
                    jnp.where(hot_z, pack_ref[dom, proj_count * atom + n : proj_count * atom + n + 1, :], 0.0)
                    for n in range(proj_count)
                ],
                axis=0,
            )
            high = values.astype(jnp.bfloat16)
            low = (values - high.astype(jnp.float32)).astype(jnp.bfloat16)
            both = jnp.concatenate([high, low], axis=0)
            boxes = lax.dot_general(hot_xy, both, (((1,), (1,)), ((), ())), preferred_element_type=jnp.float32)
            boxes = boxes + pltpu.roll(boxes, proj_count * wide, 1)
            at = dom * atom_count + atom
            low_z = home_ref[2, at] - reach
            for n in range(proj_count):
                kept = jnp.where((lane >= n * wide) & (lane < (n + 1) * wide), boxes, 0.0)
                moved = pltpu.roll(kept, lax.rem(low_z - n * wide + 2 * nz, nz), 1)
                table[at, n] = moved.reshape(box, box_y, nz)
        return carry

    field[...] = jnp.zeros_like(field)
    out[...] = jnp.zeros_like(out)
    inner = pl.ds(pad_y, ny)
    field[reach : reach + nx, pad_y : pad_y + ny, :] = orb_ref[...]
    lax.fori_loop(0, count, build, 0)

    def hamiltonian():
        def project(at, carry):
            x0, y0 = home_ref[0, at], home_ref[1, at]
            totals = [jnp.zeros((box_y, nz), jnp.float32) for _ in range(proj_count)]
            for dx in range(box):
                part = field[x0 + dx, pl.ds(y0, box_y), :]
                for n in range(proj_count):
                    totals[n] = totals[n] + table[at, n, dx] * part
            stacked = [jnp.sum(total, axis=0, keepdims=True) for total in totals]
            sums[at] = jnp.concatenate(stacked, axis=0)
            return carry

        lax.fori_loop(0, count * atom_count, project, 0)
        scaled = jnp.sum(sums[...], axis=2, keepdims=True) * coup_ref[...]
        coefs[...] = jnp.broadcast_to(scaled, coefs.shape)

        chunk = 8
        for start in range(0, nx, chunk):
            block = field[reach + start : reach + start + chunk, pad_y : pad_y + ny, :]
            z_part = jnp.dot(
                block.reshape(chunk * ny, nz), along_ref[...], precision=highest, preferred_element_type=jnp.float32
            )
            out[reach + start : reach + start + chunk, pad_y : pad_y + ny, :] = z_part.reshape(chunk, ny, nz)

        def stencil_row(row, carry):
            at = row + reach
            summed = out[at, inner, :] + pot_ref[row] * field[at, inner, :]
            for k in range(1, reach + 1):
                around = (
                    field[at + k, inner, :]
                    + field[at - k, inner, :]
                    + field[at, pl.ds(pad_y + k, ny), :]
                    + field[at, pl.ds(pad_y - k, ny), :]
                )
                summed = summed + (scale * stencil[k]) * around
            out[at, inner, :] = summed
            return carry

        lax.fori_loop(0, nx, stencil_row, 0)

        def spread(at, carry):
            x0, y0 = home_ref[0, at], home_ref[1, at]
            weights = [jnp.broadcast_to(coefs[at, n : n + 1, :], (box_y, nz)) for n in range(proj_count)]
            for dx in range(box):
                added = out[x0 + dx, pl.ds(y0, box_y), :]
                for n in range(proj_count):
                    added = added + table[at, n, dx] * weights[n]
                out[x0 + dx, pl.ds(y0, box_y), :] = added
            return carry

        lax.fori_loop(0, count * atom_count, spread, 0)

    middle = 0.5 * (top_edge + low_edge)
    half_width = 0.5 * (top_edge - low_edge)
    hamiltonian()

    def first_row(row, carry):
        at = row + reach
        field[at, inner, :] = (out[at, inner, :] - middle * field[at, inner, :]) * (1.0 / half_width)
        return carry

    lax.fori_loop(0, nx, first_row, 0)
    hamiltonian()

    def filter_row(row, carry):
        at = row + reach
        value = (out[at, inner, :] - middle * field[at, inner, :]) * (2.0 / half_width) - orb_ref[row]
        field[at, inner, :] = value
        filt_out[row] = value
        return carry

    lax.fori_loop(0, nx, filter_row, 0)
    hamiltonian()
    image_out[...] = out[reach : reach + nx, pad_y : pad_y + ny, :]


def project_kernel(
    dims,
    filt_ref,
    image_ref,
    new_out,
    res_out,
    sub_out,
    cells,
    result,
    plane,
    column,
    local_sem,
    send_sem,
    recv_sem,
    plane_send,
    plane_recv,
    column_send,
    column_recv,
    out_sem,
    pair_send,
    pair_recv,
):
    dom_x, dom_y, bands, total_cells = dims
    per_band = dom_x * dom_y
    orbs = per_band * bands
    my_x, my_y, my_band = lax.axis_index("gx"), lax.axis_index("gy"), lax.axis_index("band")
    me = my_band * per_band + my_x * dom_y + my_y
    rows = cells.shape[1] * cells.shape[2]

    def place(peer):
        inside = lax.rem(peer, per_band)
        return {"gx": inside // dom_y, "gy": lax.rem(inside, dom_y), "band": peer // per_band}

    barrier = pltpu.get_barrier_semaphore()

    def greet(step, carry):
        pl.semaphore_signal(barrier, inc=1, device_id=place(lax.rem(me + step, orbs)), device_id_type=MESH)
        return carry

    lax.fori_loop(1, orbs, greet, 0)

    def chunk_of(ref, peer):
        inside = lax.rem(peer, per_band)
        return ref.at[inside // dom_y, peer // per_band, :, lax.rem(inside, dom_y)]

    def parts(peer, source):
        return [
            pltpu.make_async_remote_copy(
                src_ref=chunk_of(ref, peer),
                dst_ref=cells.at[kind * orbs + source],
                send_sem=send_sem.at[kind, peer],
                recv_sem=recv_sem.at[kind, source],
                device_id=place(peer),
                device_id_type=MESH,
            )
            for kind, ref in enumerate((filt_ref, image_ref))
        ]

    own = [
        pltpu.make_async_copy(chunk_of(ref, me), cells.at[kind * orbs + me], local_sem.at[kind])
        for kind, ref in enumerate((filt_ref, image_ref))
    ]
    for copy in own:
        copy.start()
    pl.semaphore_wait(barrier, orbs - 1)

    def send(step, carry):
        for copy in parts(lax.rem(me + step, orbs), me):
            copy.start()
        return carry

    def finish(step, carry):
        peer = lax.rem(me + step, orbs)
        for copy in parts(peer, me):
            copy.wait_send()
        for copy in parts(peer, peer):
            copy.wait_recv()
        return carry

    lax.fori_loop(1, orbs, send, 0)
    lax.fori_loop(1, orbs, finish, 0)
    for copy in own:
        copy.wait()

    flat = cells.reshape(2 * orbs * rows, cells.shape[3])
    gram = jnp.zeros((orbs, 2 * orbs), jnp.float32)
    for row in range(rows):
        both = flat[pl.ds(row, 2 * orbs, stride=rows), :]
        gram = gram + lax.dot_general(
            both[:orbs],
            both,
            (((1,), (1,)), ((), ())),
            precision=highest,
            preferred_element_type=jnp.float32,
        )

    in_plane = dom_x * bands
    my_plane = my_x * bands + my_band
    plane[my_plane] = gram

    def plane_copy(peer, slot):
        return pltpu.make_async_remote_copy(
            src_ref=plane.at[my_plane],
            dst_ref=plane.at[slot],
            send_sem=plane_send.at[peer],
            recv_sem=plane_recv.at[slot],
            device_id={"gx": peer // bands, "gy": my_y, "band": lax.rem(peer, bands)},
            device_id_type=MESH,
        )

    for step in range(1, in_plane):
        plane_copy(lax.rem(my_plane + step, in_plane), my_plane).start()
    for step in range(1, in_plane):
        peer = lax.rem(my_plane + step, in_plane)
        plane_copy(peer, my_plane).wait_send()
        plane_copy(peer, peer).wait_recv()
    total = plane[0]
    for slot in range(1, in_plane):
        total = total + plane[slot]
    column[my_y] = total

    def column_copy(peer, slot):
        return pltpu.make_async_remote_copy(
            src_ref=column.at[my_y],
            dst_ref=column.at[slot],
            send_sem=column_send.at[peer],
            recv_sem=column_recv.at[slot],
            device_id={"gx": my_x, "gy": peer, "band": my_band},
            device_id_type=MESH,
        )

    for step in range(1, dom_y):
        column_copy(lax.rem(my_y + step, dom_y), my_y).start()
    for step in range(1, dom_y):
        peer = lax.rem(my_y + step, dom_y)
        column_copy(peer, my_y).wait_send()
        column_copy(peer, peer).wait_recv()
    total = column[0]
    for slot in range(1, dom_y):
        total = total + column[slot]
    total = total * (1.0 / total_cells)

    row_at = lax.broadcasted_iota(jnp.int32, (orbs, orbs), 0)
    col_at = lax.broadcasted_iota(jnp.int32, (orbs, orbs), 1)
    eye = jnp.where(row_at == col_at, 1.0, 0.0)
    work = jnp.concatenate([total[:, :orbs], eye], axis=1)
    row_wide = lax.broadcasted_iota(jnp.int32, (orbs, 2 * orbs), 0)
    for k in range(orbs):
        pivot_row = work[k : k + 1, :]
        pivot = work[k : k + 1, k : k + 1]
        factor = jnp.where(row_wide[:, :1] > k, work[:, k : k + 1] / pivot, 0.0)
        work = work - factor * pivot_row
    diagonal = jnp.sum(work[:, :orbs] * eye, axis=1, keepdims=True)
    inverse = work[:, orbs:] / jnp.sqrt(diagonal)

    def product(left, right, dims_in):
        return lax.dot_general(left, right, (dims_in, ((), ())), precision=highest, preferred_element_type=jnp.float32)

    projected = product(inverse, total[:, orbs:], ((1,), (0,)))
    subspace = product(projected, inverse, ((1,), (1,)))
    sub_out[...] = subspace
    half_width = 0.5 * (top_edge - low_edge)
    mixed = product(subspace, inverse, ((0,), (0,))) * (-1.0 / half_width)
    top = jnp.concatenate([inverse, jnp.zeros_like(inverse)], axis=1)
    bottom = jnp.concatenate([mixed, inverse * (1.0 / half_width)], axis=1)
    rotation = jnp.concatenate([top, bottom], axis=0)
    flat_result = result.reshape(2 * orbs * rows, cells.shape[3])
    for row in range(rows):
        both = flat[pl.ds(row, 2 * orbs, stride=rows), :]
        flat_result[pl.ds(row, 2 * orbs, stride=rows), :] = product(rotation, both, ((1,), (0,)))

    outs = (new_out, res_out)
    keep = [
        pltpu.make_async_copy(
            result.at[pl.ds(kind * orbs + my_band * per_band, per_band)], out.at[:, my_band], out_sem.at[kind]
        )
        for kind, out in enumerate(outs)
    ]
    for copy in keep:
        copy.start()

    def pair_copy(kind, other, half):
        return pltpu.make_async_remote_copy(
            src_ref=result.at[pl.ds(kind * orbs + other * per_band, per_band)],
            dst_ref=outs[kind].at[:, half],
            send_sem=pair_send.at[kind, other],
            recv_sem=pair_recv.at[kind, half],
            device_id={"gx": my_x, "gy": my_y, "band": other},
            device_id_type=MESH,
        )

    for step in range(1, bands):
        other = lax.rem(my_band + step, bands)
        for kind in range(2):
            pair_copy(kind, other, my_band).start()
    for step in range(1, bands):
        other = lax.rem(my_band + step, bands)
        for kind in range(2):
            pair_copy(kind, other, my_band).wait_send()
            pair_copy(kind, other, other).wait_recv()
    for copy in keep:
        copy.wait()


def per_device_whole(orbitals, local_potential, atom_cell, support_offset, projector, coupling):
    orb_count, size_x, size_y, nz = orbitals.shape
    dom_x, dom_y, bands = lax.axis_size("gx"), lax.axis_size("gy"), lax.axis_size("band")
    count = dom_x * dom_y
    nx, ny = dom_x * size_x, dom_y * size_y
    atom_count, proj_count, points = projector.shape[2:]
    atoms = count * atom_count
    any_spec = pl.BlockSpec(memory_space=pl.ANY)
    vmem = pl.BlockSpec(memory_space=pltpu.VMEM)
    smem = pl.BlockSpec(memory_space=pltpu.SMEM)

    cell = atom_cell[0, 0]
    offset = support_offset[:, 0, 0]
    home_z = cell % nz
    point_z = home_z[:, None] + offset[2]
    box_cell = ((offset[0] + reach) * box_y + offset[1] + reach) * 16 + offset[2] + reach
    box_cell = jnp.where((point_z >= 0) & (point_z < nz), box_cell, -1).astype(jnp.float32)
    small = jnp.concatenate([coupling[0, 0].reshape(-1), cell.astype(jnp.float32)])
    pack = jnp.concatenate(
        [
            projector[0, 0].reshape(atom_count * proj_count, points),
            box_cell,
            jnp.pad(small, (0, points - small.shape[0]))[None],
            jnp.zeros((16 - atom_count * proj_count - atom_count - 1, points), jnp.float32),
        ],
        axis=0,
    )
    f32 = jnp.float32
    whole_orb, whole_pot, packs = pl.pallas_call(
        functools.partial(gather_kernel, (dom_x, dom_y)),
        out_shape=(
            jax.ShapeDtypeStruct((dom_x, size_x, dom_y, size_y, nz), f32),
            jax.ShapeDtypeStruct((dom_x, size_x, dom_y, size_y, nz), f32),
            jax.ShapeDtypeStruct((count, 16, points), f32),
        ),
        in_specs=[any_spec] * 3,
        out_specs=(any_spec,) * 3,
        scratch_shapes=[
            pltpu.SemaphoreType.DMA((3,)),
            pltpu.SemaphoreType.DMA((3, count)),
            pltpu.SemaphoreType.DMA((3, count)),
        ],
        compiler_params=pltpu.CompilerParams(collective_id=0, has_side_effects=True),
    )(orbitals, local_potential, pack)

    smalls = packs[:, atom_count * proj_count + atom_count, :]
    coups = smalls[:, : atom_count * proj_count].reshape(atoms, proj_count, 1)
    homes = smalls[:, atom_count * proj_count : atom_count * proj_count + atom_count].astype(jnp.int32)
    dom = jnp.arange(count, dtype=jnp.int32)[:, None]
    home_x = dom // dom_y * size_x + homes // (size_y * nz)
    home_y = dom % dom_y * size_y + homes // nz % size_y + pad_y - reach
    home = jnp.stack([home_x.reshape(-1), home_y.reshape(-1), (homes % nz).reshape(-1)])
    along = np.zeros((nz, nz), np.float32)
    for i in range(nz):
        for j in range(max(0, i - reach), min(nz, i + reach + 1)):
            along[i, j] = scale * stencil[abs(i - j)] * (3.0 if i == j else 1.0)

    field_shape = (nx + 2 * reach, ny + 2 * pad_y + 8, nz)
    filt, image = pl.pallas_call(
        functools.partial(compute_kernel, (count, atom_count, proj_count)),
        out_shape=(jax.ShapeDtypeStruct((nx, ny, nz), f32),) * 2,
        in_specs=[smem] + [vmem] * 5,
        out_specs=(vmem, vmem),
        scratch_shapes=[
            pltpu.VMEM((atoms, proj_count, box, box_y, nz), f32),
            pltpu.VMEM(field_shape, f32),
            pltpu.VMEM(field_shape, f32),
            pltpu.VMEM((atoms, proj_count, nz), f32),
            pltpu.VMEM((atoms, proj_count, nz), f32),
        ],
        compiler_params=pltpu.CompilerParams(vmem_limit_bytes=48 << 20),
    )(home, whole_orb.reshape(nx, ny, nz), whole_pot.reshape(nx, ny, nz), packs, coups, jnp.asarray(along))

    orbs = orb_count * bands
    half = size_x // bands
    rows = half * size_y
    shape = (dom_x, bands, half, dom_y, size_y, nz)
    sem = pltpu.SemaphoreType.DMA
    new, res, sub = pl.pallas_call(
        functools.partial(project_kernel, (dom_x, dom_y, bands, float(nx * ny * nz))),
        out_shape=(
            jax.ShapeDtypeStruct((orb_count, bands, half, size_y, nz), f32),
            jax.ShapeDtypeStruct((orb_count, bands, half, size_y, nz), f32),
            jax.ShapeDtypeStruct((orbs, orbs), f32),
        ),
        in_specs=[any_spec] * 2,
        out_specs=(any_spec, any_spec, vmem),
        scratch_shapes=[
            pltpu.VMEM((2 * orbs, half, size_y, nz), f32),
            pltpu.VMEM((2 * orbs, half, size_y, nz), f32),
            pltpu.VMEM((dom_x * bands, orbs, 2 * orbs), f32),
            pltpu.VMEM((dom_y, orbs, 2 * orbs), f32),
            sem((2,)),
            sem((2, orbs)),
            sem((2, orbs)),
            sem((dom_x * bands,)),
            sem((dom_x * bands,)),
            sem((dom_y,)),
            sem((dom_y,)),
            sem((2,)),
            sem((2, bands)),
            sem((2, bands)),
        ],
        compiler_params=pltpu.CompilerParams(
            collective_id=1, has_side_effects=True, vmem_limit_bytes=32 << 20
        ),
    )(filt.reshape(shape), image.reshape(shape))
    return (new.reshape(orbitals.shape), res.reshape(orbitals.shape), sub)


def per_device(orbitals, local_potential, atom_cell, support_offset, projector, coupling):
    domains = lax.axis_size("gx") * lax.axis_size("gy")
    if orbitals.shape[0] == domains and orbitals.shape[1] % lax.axis_size("band") == 0:
        plan = per_device_whole
    else:
        plan = per_device_halo
    return plan(orbitals, local_potential, atom_cell, support_offset, projector, coupling)


def solution(mesh):
    in_specs = (
        P("band", "gx", "gy", None),
        P("gx", "gy", None),
        P("gx", "gy", None),
        P(None, "gx", "gy", None, None),
        P("gx", "gy", None, None, None),
        P("gx", "gy", None, None),
    )
    out_specs = (P("band", "gx", "gy", None), P("band", "gx", "gy", None), P())
    return jax.shard_map(
        per_device, mesh=mesh, in_specs=in_specs, out_specs=out_specs, check_vma=False
    )
```

```python
import functools

import jax
import jax.numpy as jnp
import numpy as np
from jax import lax
from jax.experimental import pallas as pl
from jax.experimental.pallas import tpu as pltpu
from jax.sharding import PartitionSpec as P

spacing = 0.4
low_edge = 6.0
top_edge = 150.0
stencil = (
    -5369.0 / 1800.0,
    12.0 / 7.0,
    -15.0 / 56.0,
    10.0 / 189.0,
    -1.0 / 112.0,
    2.0 / 1925.0,
    -1.0 / 16632.0,
)
highest = lax.Precision.HIGHEST


def with_halo(cells, sides, width):
    for axis, dim in sides:
        count = lax.axis_size(axis)
        ends = count - 1
        head = lax.slice_in_dim(cells, 0, width, axis=dim)
        tail = lax.slice_in_dim(cells, cells.shape[dim] - width, cells.shape[dim], axis=dim)
        cells = jnp.concatenate(
            [
                lax.ppermute(tail, axis, [(i, (i + 1) % count) for i in range(ends)]),
                cells,
                lax.ppermute(head, axis, [((i + 1) % count, i) for i in range(ends)]),
            ],
            axis=dim,
        )
    return cells


def kinetic_part(extended, orbital_block):
    size_x, size_y, size_z = (
        orbital_block.shape[1],
        orbital_block.shape[2],
        orbital_block.shape[3],
    )
    padded_z = jnp.pad(orbital_block, ((0, 0), (0, 0), (0, 0), (6, 6)))
    summed = 3.0 * stencil[0] * orbital_block
    for stride in range(1, 7):
        along_x = (
            extended[:, 6 + stride : 6 + stride + size_x, 6 : 6 + size_y]
            + extended[:, 6 - stride : 6 - stride + size_x, 6 : 6 + size_y]
        )
        along_y = (
            extended[:, 6 : 6 + size_x, 6 + stride : 6 + stride + size_y]
            + extended[:, 6 : 6 + size_x, 6 - stride : 6 - stride + size_y]
        )
        along_z = (
            padded_z[..., 6 + stride : 6 + stride + size_z]
            + padded_z[..., 6 - stride : 6 - stride + size_z]
        )
        summed = summed + stencil[stride] * (along_x + along_y + along_z)
    return -0.5 / spacing**2 * summed


def prepare_tables(atom_cell, support_offset, projector, size_x, size_y, size_z):
    home_cell = atom_cell[..., None]
    relative = jnp.stack(
        [
            home_cell // (size_y * size_z) + support_offset[0],
            home_cell // size_z % size_y + support_offset[1],
            home_cell % size_z + support_offset[2],
        ]
    )
    rel_near = with_halo(relative, (("gx", 1), ("gy", 2)), 1)
    beta_near = with_halo(projector, (("gx", 0), ("gy", 1)), 1)
    atom_count, proj_count = (projector.shape[2], projector.shape[3])
    cell_count = size_x * size_y * size_z
    frame_x = (lax.broadcasted_iota(jnp.int32, (3, 3, 1, 1), 0) - 1) * size_x
    frame_y = (lax.broadcasted_iota(jnp.int32, (3, 3, 1, 1), 1) - 1) * size_y
    coord_x = rel_near[0] + frame_x
    coord_y = rel_near[1] + frame_y
    coord_z = rel_near[2]
    inside = (
        (coord_x >= 0)
        & (coord_x < size_x)
        & (coord_y >= 0)
        & (coord_y < size_y)
        & (coord_z >= 0)
        & (coord_z < size_z)
    ).astype(jnp.float32)
    cell_index = (
        jnp.clip(coord_x, 0, size_x - 1) * size_y + jnp.clip(coord_y, 0, size_y - 1)
    ) * size_z + jnp.clip(coord_z, 0, size_z - 1)
    near_columns = jnp.arange(9 * atom_count * proj_count, dtype=jnp.int32).reshape(
        3, 3, atom_count, proj_count, 1
    )
    near_flat = near_columns * cell_count + cell_index[:, :, :, None, :]
    near_values = beta_near * inside[:, :, :, None, :]
    table_near = (
        jnp.zeros((9 * atom_count * proj_count * cell_count,), jnp.float32)
        .at[near_flat.reshape(-1)]
        .add(near_values.reshape(-1))
    )
    table_near = table_near.reshape(3, 3, atom_count, proj_count, cell_count)
    own_rel = relative[:, 0, 0]
    own_x = own_rel[0] + 6
    own_y = own_rel[1] + 6
    own_z = own_rel[2]
    own_zin = ((own_z >= 0) & (own_z < size_z)).astype(jnp.float32)
    own_index = (own_x * (size_y + 12) + own_y) * size_z + jnp.clip(own_z, 0, size_z - 1)
    ext_count = (size_x + 12) * (size_y + 12) * size_z
    own_columns = jnp.arange(atom_count * proj_count, dtype=jnp.int32).reshape(
        atom_count, proj_count, 1
    )
    own_flat = own_columns * ext_count + own_index[:, None, :]
    own_values = projector[0, 0] * own_zin[:, None, :]
    table_own = (
        jnp.zeros((atom_count * proj_count * ext_count,), jnp.float32)
        .at[own_flat.reshape(-1)]
        .add(own_values.reshape(-1))
    )
    table_own = table_own.reshape(atom_count, proj_count, ext_count)
    return (table_near, table_own)


def apply_hamiltonian(orbital_block, local_potential, tables, coupling_own):
    table_near, table_own = tables
    orb_count = orbital_block.shape[0]
    atom_count, proj_count = coupling_own.shape
    flat_block = orbital_block.reshape(orb_count, -1)
    extended = with_halo(orbital_block, (("gx", 1), ("gy", 2)), 6)
    kinetic = kinetic_part(extended, orbital_block)
    partial_terms = jnp.einsum("ijanc,bc->ijanb", table_near, flat_block, precision=highest)
    received = with_halo(partial_terms.reshape(1, 1, -1), (("gx", 0), ("gy", 1)), 1)
    grouped = received.reshape(3, 3, 3, 3, atom_count, proj_count, orb_count)
    coefficients = grouped[1, 1, 1, 1]
    for row_pos in range(3):
        for col_pos in range(3):
            if row_pos != 1 or col_pos != 1:
                coefficients = coefficients + grouped[row_pos, col_pos, 2 - row_pos, 2 - col_pos]
    scaled = coupling_own[:, :, None] * coefficients
    near_coefs = with_halo(scaled.reshape(1, 1, -1), (("gx", 0), ("gy", 1)), 1)
    near_coefs = near_coefs.reshape(3, 3, atom_count, proj_count, orb_count)
    projector_term = jnp.einsum("ijanc,ijanb->bc", table_near, near_coefs, precision=highest)
    return kinetic + local_potential * orbital_block + projector_term.reshape(orbital_block.shape)


def inverse_factor(intersection):
    factor = jnp.linalg.cholesky(intersection)
    identity = jnp.eye(intersection.shape[0], dtype=jnp.float32)
    return lax.linalg.triangular_solve(factor, identity, left_side=True, lower=True)


def per_device_halo(orbitals, local_potential, atom_cell, support_offset, projector, coupling):
    orb_count, size_x, size_y, size_z = orbitals.shape
    tables = prepare_tables(atom_cell, support_offset, projector, size_x, size_y, size_z)
    coupling_own = coupling[0, 0]

    def hamiltonian(orbital_block):
        return apply_hamiltonian(orbital_block, local_potential, tables, coupling_own)

    middle = 0.5 * (top_edge + low_edge)
    half_width = 0.5 * (top_edge - low_edge)
    total_cells = float(size_x * size_y * size_z * lax.axis_size("gx") * lax.axis_size("gy"))
    band_start = lax.axis_index("band") * orb_count
    first_term = (hamiltonian(orbitals) - middle * orbitals) / half_width
    filtered = 2.0 * (hamiltonian(first_term) - middle * first_term) / half_width - orbitals
    filt_flat = filtered.reshape(orb_count, -1)
    orbs_all = orb_count * lax.axis_size("band")
    empty_square = jnp.zeros((orbs_all, orbs_all), jnp.float32)
    whole_block = lax.all_gather(filt_flat, "band", axis=0, tiled=True)
    over_cols = jnp.einsum("kc,lc->kl", whole_block, filt_flat, precision=highest) / total_cells
    intersection = lax.psum(
        lax.dynamic_update_slice(empty_square, over_cols, (0, band_start)), ("gx", "gy", "band")
    )
    inverse = inverse_factor(intersection)
    rotated_all = jnp.dot(inverse, whole_block, precision=highest)
    rotated = lax.dynamic_slice_in_dim(rotated_all, band_start, orb_count, 0)
    image_own = hamiltonian(rotated.reshape(orbitals.shape)).reshape(orb_count, -1)
    sub_cols = jnp.einsum("kc,lc->kl", rotated_all, image_own, precision=highest) / total_cells
    subspace = lax.psum(
        lax.dynamic_update_slice(empty_square, sub_cols, (0, band_start)), ("gx", "gy", "band")
    )
    cols_own = lax.dynamic_slice_in_dim(subspace, band_start, orb_count, 1)
    residual = (
        image_own - jnp.einsum("kl,kc->lc", cols_own, rotated_all, precision=highest)
    ) / half_width
    return (rotated.reshape(orbitals.shape), residual.reshape(orbitals.shape), subspace)


MESH = pl.DeviceIdType.MESH
reach = 6
box = 2 * reach + 1
box_y = 16
pad_y = 8
scale = -0.5 / spacing**2


def gather_kernel(
    dims, orb_ref, pot_ref, pack_ref, orb_out, pot_out, pack_out, local_sem, send_sem, recv_sem, *stage_sems
):
    dom_x, dom_y, bands = dims
    count = dom_x * dom_y
    my_x, my_y, my_band = lax.axis_index("gx"), lax.axis_index("gy"), lax.axis_index("band")
    me = my_x * dom_y + my_y
    half = pot_ref.shape[0] // bands
    mine = pl.ds(my_band * half, half)

    barrier = pltpu.get_barrier_semaphore()

    def greet(step, carry):
        peer = lax.rem(me + step, count)
        pl.semaphore_signal(
            barrier, inc=1, device_id={"gx": peer // dom_y, "gy": lax.rem(peer, dom_y)}, device_id_type=MESH
        )
        return carry

    lax.fori_loop(1, count, greet, 0)
    for step in range(1, bands):
        pl.semaphore_signal(
            barrier, inc=1, device_id={"band": lax.rem(my_band + step, bands)}, device_id_type=MESH
        )

    def orb_copy(peer, source):
        return pltpu.make_async_remote_copy(
            src_ref=orb_ref.at[peer],
            dst_ref=orb_out.at[source // dom_y, :, lax.rem(source, dom_y)],
            send_sem=send_sem.at[peer],
            recv_sem=recv_sem.at[source],
            device_id={"gx": peer // dom_y, "gy": lax.rem(peer, dom_y)},
            device_id_type=MESH,
        )

    def stage_copies(stage, axis, peer, source):
        if stage == 0:
            pairs = (
                (pack_ref.at[my_band], pack_out.at[my_x * dom_y + source, my_band]),
                (pot_ref.at[mine], pot_out.at[my_x, mine, source]),
            )
        elif stage == 1:
            block = pack_out.at[pl.ds(source * dom_y, dom_y), my_band]
            strip = pot_out.at[source, mine]
            pairs = ((block, block), (strip, strip))
        else:
            block = pack_out.at[:, source]
            strip = pot_out.at[:, pl.ds(source * half, half)]
            pairs = ((block, block), (strip, strip))
        return [
            pltpu.make_async_remote_copy(
                src_ref=src,
                dst_ref=dst,
                send_sem=stage_sems[2 * stage].at[kind, peer],
                recv_sem=stage_sems[2 * stage + 1].at[kind, source],
                device_id={axis: peer},
                device_id_type=MESH,
            )
            for kind, (src, dst) in enumerate(pairs)
        ]

    def start_stage(stage, axis, place, size):
        for step in range(1, size):
            for copy in stage_copies(stage, axis, lax.rem(place + step, size), place):
                copy.start()

    def end_stage(stage, axis, place, size):
        for step in range(1, size):
            peer = lax.rem(place + step, size)
            for copy in stage_copies(stage, axis, peer, place):
                copy.wait_send()
            for copy in stage_copies(stage, axis, peer, peer):
                copy.wait_recv()

    own = [
        pltpu.make_async_copy(pack_ref.at[my_band], pack_out.at[me, my_band], local_sem.at[0]),
        pltpu.make_async_copy(pot_ref.at[mine], pot_out.at[my_x, mine, my_y], local_sem.at[1]),
        pltpu.make_async_copy(orb_ref.at[me], orb_out.at[my_x, :, my_y], local_sem.at[2]),
    ]
    for copy in own:
        copy.start()
    pl.semaphore_wait(barrier, count - 1 + bands - 1)

    def send(step, carry):
        orb_copy(lax.rem(me + step, count), me).start()
        return carry

    def finish(step, carry):
        peer = lax.rem(me + step, count)
        orb_copy(peer, me).wait_send()
        orb_copy(peer, peer).wait_recv()
        return carry

    early = count // 4
    start_stage(0, "gy", my_y, dom_y)
    lax.fori_loop(1, early, send, 0)
    end_stage(0, "gy", my_y, dom_y)
    own[0].wait()
    own[1].wait()
    start_stage(1, "gx", my_x, dom_x)
    lax.fori_loop(early, count, send, 0)
    end_stage(1, "gx", my_x, dom_x)
    start_stage(2, "band", my_band, bands)
    end_stage(2, "band", my_band, bands)
    lax.fori_loop(1, count, finish, 0)
    own[2].wait()


def compute_kernel(
    dims,
    orb_any,
    pot_any,
    pack_any,
    along_ref,
    filt_any,
    image_any,
    table,
    field,
    out,
    sums,
    coefs,
    orb_ref,
    pot_ref,
    pack_ref,
    small,
    copy_sem,
):
    count, atom_count, proj_count, dom_y, size_x, size_y = dims
    nx, ny, nz = orb_ref.shape
    points = pack_ref.shape[3]
    fetch_pack = pltpu.make_async_copy(pack_any, pack_ref, copy_sem.at[0])
    fetch_small = pltpu.make_async_copy(pack_any.at[:, :, proj_count + 1, pl.ds(0, 128)], small, copy_sem.at[1])
    fetch_pack.start()
    fetch_small.start()
    field[...] = jnp.zeros_like(field)
    inside_field = field.at[pl.ds(reach, nx), pl.ds(pad_y, ny), :]
    fetch_field = pltpu.make_async_copy(orb_any, inside_field, copy_sem.at[2])
    fetch_pot = pltpu.make_async_copy(pot_any, pot_ref, copy_sem.at[3])
    fetch_orb = pltpu.make_async_copy(orb_any, orb_ref, copy_sem.at[4])
    fetch_field.start()
    fetch_pot.start()
    fetch_orb.start()

    def home_of(dom, atom):
        cell = small[dom, atom, proj_count].astype(jnp.int32)
        home_x = dom // dom_y * size_x + cell // (size_y * nz)
        home_y = lax.rem(dom, dom_y) * size_y + lax.rem(cell // nz, size_y) + pad_y - reach
        return home_x, home_y, lax.rem(cell, nz)

    rows = box * box_y
    wide = 16
    lane = lax.broadcasted_iota(jnp.int32, (rows, nz), 1)
    row_xy = lax.broadcasted_iota(jnp.int32, (rows, points), 0)
    row_z = lax.broadcasted_iota(jnp.int32, (wide, points), 0)

    def build(dom, carry):
        for atom in range(atom_count):
            cell = pack_ref[dom, atom, proj_count : proj_count + 1, :].astype(jnp.int32)
            hot_xy = jnp.where(row_xy == lax.shift_right_arithmetic(cell, 4), 1.0, 0.0).astype(jnp.bfloat16)
            hot_z = row_z == (cell & 15)
            values = jnp.concatenate(
                [
                    jnp.where(hot_z, pack_ref[dom, atom, n : n + 1, :], 0.0)
                    for n in range(proj_count)
                ],
                axis=0,
            )
            high = values.astype(jnp.bfloat16)
            low = (values - high.astype(jnp.float32)).astype(jnp.bfloat16)
            both = jnp.concatenate([high, low], axis=0)
            boxes = lax.dot_general(hot_xy, both, (((1,), (1,)), ((), ())), preferred_element_type=jnp.float32)
            boxes = boxes + pltpu.roll(boxes, proj_count * wide, 1)
            at = dom * atom_count + atom
            low_z = home_of(dom, atom)[2] - reach
            for n in range(proj_count):
                kept = jnp.where((lane >= n * wide) & (lane < (n + 1) * wide), boxes, 0.0)
                moved = pltpu.roll(kept, lax.rem(low_z - n * wide + 2 * nz, nz), 1)
                table[at, n] = moved.reshape(box, box_y, nz)
        return carry

    out[...] = jnp.zeros_like(out)
    inner = pl.ds(pad_y, ny)
    fetch_pack.wait()
    fetch_small.wait()
    lax.fori_loop(0, count, build, 0)
    fetch_field.wait()
    fetch_pot.wait()
    fetch_orb.wait()

    def hamiltonian():
        def project(at, carry):
            x0, y0, _ = home_of(at // atom_count, lax.rem(at, atom_count))
            totals = [jnp.zeros((box_y, nz), jnp.float32) for _ in range(proj_count)]
            for dx in range(box):
                part = field[x0 + dx, pl.ds(y0, box_y), :]
                for n in range(proj_count):
                    totals[n] = totals[n] + table[at, n, dx] * part
            stacked = [jnp.sum(total, axis=0, keepdims=True) for total in totals]
            sums[at] = jnp.concatenate(stacked, axis=0)
            return carry

        lax.fori_loop(0, count * atom_count, project, 0)
        scaled = jnp.sum(sums[...], axis=2, keepdims=True)
        coefs[...] = jnp.broadcast_to(scaled, coefs.shape)

        chunk = 8
        for start in range(0, nx, chunk):
            block = field[reach + start : reach + start + chunk, pad_y : pad_y + ny, :]
            z_part = jnp.dot(
                block.reshape(chunk * ny, nz), along_ref[...], precision=highest, preferred_element_type=jnp.float32
            )
            out[reach + start : reach + start + chunk, pad_y : pad_y + ny, :] = z_part.reshape(chunk, ny, nz)

        def stencil_row(row, carry):
            at = row + reach
            summed = out[at, inner, :] + pot_ref[row] * field[at, inner, :]
            for k in range(1, reach + 1):
                around = (
                    field[at + k, inner, :]
                    + field[at - k, inner, :]
                    + field[at, pl.ds(pad_y + k, ny), :]
                    + field[at, pl.ds(pad_y - k, ny), :]
                )
                summed = summed + (scale * stencil[k]) * around
            out[at, inner, :] = summed
            return carry

        lax.fori_loop(0, nx, stencil_row, 0)

        def spread(at, carry):
            x0, y0, _ = home_of(at // atom_count, lax.rem(at, atom_count))
            weights = [
                jnp.broadcast_to(
                    coefs[at, n : n + 1, :] * small[at // atom_count, lax.rem(at, atom_count), n], (box_y, nz)
                )
                for n in range(proj_count)
            ]
            for dx in range(box):
                added = out[x0 + dx, pl.ds(y0, box_y), :]
                for n in range(proj_count):
                    added = added + table[at, n, dx] * weights[n]
                out[x0 + dx, pl.ds(y0, box_y), :] = added
            return carry

        lax.fori_loop(0, count * atom_count, spread, 0)

    middle = 0.5 * (top_edge + low_edge)
    half_width = 0.5 * (top_edge - low_edge)
    hamiltonian()

    def first_row(row, carry):
        at = row + reach
        field[at, inner, :] = (out[at, inner, :] - middle * field[at, inner, :]) * (1.0 / half_width)
        return carry

    lax.fori_loop(0, nx, first_row, 0)
    hamiltonian()

    def filter_row(row, carry):
        at = row + reach
        value = (out[at, inner, :] - middle * field[at, inner, :]) * (2.0 / half_width) - orb_ref[row]
        field[at, inner, :] = value
        orb_ref[row] = value
        return carry

    lax.fori_loop(0, nx, filter_row, 0)
    store_filt = pltpu.make_async_copy(orb_ref, filt_any, copy_sem.at[5])
    store_filt.start()
    hamiltonian()
    store_image = pltpu.make_async_copy(out.at[pl.ds(reach, nx), pl.ds(pad_y, ny), :], image_any, copy_sem.at[6])
    store_image.start()
    store_filt.wait()
    store_image.wait()


def project_kernel(
    dims,
    filt_ref,
    image_ref,
    new_out,
    res_out,
    sub_out,
    cells,
    result,
    plane,
    column,
    local_sem,
    send_sem,
    recv_sem,
    plane_send,
    plane_recv,
    column_send,
    column_recv,
    out_sem,
    pair_send,
    pair_recv,
):
    dom_x, dom_y, bands, total_cells = dims
    per_band = dom_x * dom_y
    orbs = per_band * bands
    my_x, my_y, my_band = lax.axis_index("gx"), lax.axis_index("gy"), lax.axis_index("band")
    me = my_band * per_band + my_x * dom_y + my_y
    rows = cells.shape[1] * cells.shape[2]

    def place(peer):
        inside = lax.rem(peer, per_band)
        return {"gx": inside // dom_y, "gy": lax.rem(inside, dom_y), "band": peer // per_band}

    barrier = pltpu.get_barrier_semaphore()

    def greet(step, carry):
        pl.semaphore_signal(barrier, inc=1, device_id=place(lax.rem(me + step, orbs)), device_id_type=MESH)
        return carry

    lax.fori_loop(1, orbs, greet, 0)

    def chunk_of(ref, peer):
        inside = lax.rem(peer, per_band)
        return ref.at[inside // dom_y, peer // per_band, :, lax.rem(inside, dom_y)]

    def parts(peer, source):
        return [
            pltpu.make_async_remote_copy(
                src_ref=chunk_of(ref, peer),
                dst_ref=cells.at[kind * orbs + source],
                send_sem=send_sem.at[kind, peer],
                recv_sem=recv_sem.at[kind, source],
                device_id=place(peer),
                device_id_type=MESH,
            )
            for kind, ref in enumerate((filt_ref, image_ref))
        ]

    own = [
        pltpu.make_async_copy(chunk_of(ref, me), cells.at[kind * orbs + me], local_sem.at[kind])
        for kind, ref in enumerate((filt_ref, image_ref))
    ]
    for copy in own:
        copy.start()
    pl.semaphore_wait(barrier, orbs - 1)

    for kind in range(2):

        def send(step, carry, kind=kind):
            parts(lax.rem(me + step, orbs), me)[kind].start()
            return carry

        lax.fori_loop(1, orbs, send, 0)

    def finish(kind):
        def one(step, carry):
            peer = lax.rem(me + step, orbs)
            parts(peer, me)[kind].wait_send()
            parts(peer, peer)[kind].wait_recv()
            return carry

        lax.fori_loop(1, orbs, one, 0)
        own[kind].wait()

    flat = cells.reshape(2 * orbs * rows, cells.shape[3])
    flat_result = result.reshape(2 * orbs * rows, cells.shape[3])

    def product(left, right, dims_in):
        return lax.dot_general(left, right, (dims_in, ((), ())), precision=highest, preferred_element_type=jnp.float32)

    def load(ref, kind, row):
        return ref[pl.ds(kind * orbs * rows + row, orbs, stride=rows), :]

    in_plane = dom_x * bands
    my_plane = my_x * bands + my_band

    def plane_copy(kind, peer, slot):
        return pltpu.make_async_remote_copy(
            src_ref=plane.at[kind, my_plane],
            dst_ref=plane.at[kind, slot],
            send_sem=plane_send.at[kind, peer],
            recv_sem=plane_recv.at[kind, slot],
            device_id={"gx": peer // bands, "gy": my_y, "band": lax.rem(peer, bands)},
            device_id_type=MESH,
        )

    def column_copy(kind, peer, slot):
        return pltpu.make_async_remote_copy(
            src_ref=column.at[kind, my_y],
            dst_ref=column.at[kind, slot],
            send_sem=column_send.at[kind, peer],
            recv_sem=column_recv.at[kind, slot],
            device_id={"gx": my_x, "gy": peer, "band": my_band},
            device_id_type=MESH,
        )

    def summed(kind, share, box_ref, copy_of, place_at, size):
        box_ref[kind, place_at] = share
        for step in range(1, size):
            copy_of(kind, lax.rem(place_at + step, size), place_at).start()
        for step in range(1, size):
            peer = lax.rem(place_at + step, size)
            copy_of(kind, peer, place_at).wait_send()
            copy_of(kind, peer, peer).wait_recv()
        total = box_ref[kind, 0]
        for slot in range(1, size):
            total = total + box_ref[kind, slot]
        return total

    def all_sum(kind, share):
        share = summed(kind, share, plane, plane_copy, my_plane, in_plane)
        return summed(kind, share, column, column_copy, my_y, dom_y) * (1.0 / total_cells)

    finish(0)
    gram = jnp.zeros((orbs, orbs), jnp.float32)
    for row in range(rows):
        part = load(flat, 0, row)
        gram = gram + product(part, part, ((1,), (1,)))
    total = all_sum(0, gram)

    row_at = lax.broadcasted_iota(jnp.int32, (orbs, orbs), 0)
    col_at = lax.broadcasted_iota(jnp.int32, (orbs, orbs), 1)
    eye = jnp.where(row_at == col_at, 1.0, 0.0)
    work = jnp.concatenate([total, eye], axis=1)
    row_wide = lax.broadcasted_iota(jnp.int32, (orbs, 2 * orbs), 0)
    for k in range(orbs):
        pivot_row = work[k : k + 1, :]
        pivot = work[k : k + 1, k : k + 1]
        factor = jnp.where(row_wide[:, :1] > k, work[:, k : k + 1] / pivot, 0.0)
        work = work - factor * pivot_row
    diagonal = jnp.sum(work[:, :orbs] * eye, axis=1, keepdims=True)
    inverse = work[:, orbs:] / jnp.sqrt(diagonal)

    outs = (new_out, res_out)

    def pair_copy(kind, other, half):
        return pltpu.make_async_remote_copy(
            src_ref=result.at[pl.ds(kind * orbs + other * per_band, per_band)],
            dst_ref=outs[kind].at[:, half],
            send_sem=pair_send.at[kind, other],
            recv_sem=pair_recv.at[kind, half],
            device_id={"gx": my_x, "gy": my_y, "band": other},
            device_id_type=MESH,
        )

    def keep(kind):
        source = result.at[pl.ds(kind * orbs + my_band * per_band, per_band)]
        return pltpu.make_async_copy(source, outs[kind].at[:, my_band], out_sem.at[kind])

    def give(kind):
        for step in range(1, bands):
            pair_copy(kind, lax.rem(my_band + step, bands), my_band).start()
        keep(kind).start()

    for row in range(rows):
        flat_result[pl.ds(row, orbs, stride=rows), :] = product(inverse, load(flat, 0, row), ((1,), (0,)))
    give(0)

    finish(1)
    gram = jnp.zeros((orbs, orbs), jnp.float32)
    for row in range(rows):
        gram = gram + product(load(flat, 0, row), load(flat, 1, row), ((1,), (1,)))
    total = all_sum(1, gram)
    projected = product(inverse, total, ((1,), (0,)))
    subspace = product(projected, inverse, ((1,), (1,)))
    sub_out[...] = subspace
    half_width = 0.5 * (top_edge - low_edge)
    mixed = product(subspace, inverse, ((0,), (0,))) * (-1.0 / half_width)
    rotation = jnp.concatenate([mixed, inverse * (1.0 / half_width)], axis=1)
    for row in range(rows):
        both = jnp.concatenate([load(flat, 0, row), load(flat, 1, row)], axis=0)
        flat_result[pl.ds(orbs * rows + row, orbs, stride=rows), :] = product(rotation, both, ((1,), (0,)))
    give(1)

    for kind in range(2):
        for step in range(1, bands):
            other = lax.rem(my_band + step, bands)
            pair_copy(kind, other, my_band).wait_send()
            pair_copy(kind, other, other).wait_recv()
        keep(kind).wait()


def per_device_whole(orbitals, local_potential, atom_cell, support_offset, projector, coupling):
    orb_count, size_x, size_y, nz = orbitals.shape
    dom_x, dom_y, bands = lax.axis_size("gx"), lax.axis_size("gy"), lax.axis_size("band")
    count = dom_x * dom_y
    nx, ny = dom_x * size_x, dom_y * size_y
    atom_count, proj_count, points = projector.shape[2:]
    atoms = count * atom_count
    any_spec = pl.BlockSpec(memory_space=pl.ANY)
    vmem = pl.BlockSpec(memory_space=pltpu.VMEM)

    cell = atom_cell[0, 0]
    offset = support_offset[:, 0, 0]
    home_z = cell % nz
    point_z = home_z[:, None] + offset[2]
    box_cell = ((offset[0] + reach) * box_y + offset[1] + reach) * 16 + offset[2] + reach
    box_cell = jnp.where((point_z >= 0) & (point_z < nz), box_cell, -1).astype(jnp.float32)
    small = jnp.concatenate([coupling[0, 0], cell[:, None].astype(jnp.float32)], axis=1)
    pack = jnp.concatenate(
        [
            projector[0, 0],
            box_cell[:, None],
            jnp.pad(small, ((0, 0), (0, points - small.shape[1])))[:, None],
            jnp.zeros((atom_count, 8 - proj_count - 2, points), jnp.float32),
        ],
        axis=1,
    )
    f32 = jnp.float32
    whole_orb, whole_pot, packs = pl.pallas_call(
        functools.partial(gather_kernel, (dom_x, dom_y, bands)),
        out_shape=(
            jax.ShapeDtypeStruct((dom_x, size_x, dom_y, size_y, nz), f32),
            jax.ShapeDtypeStruct((dom_x, size_x, dom_y, size_y, nz), f32),
            jax.ShapeDtypeStruct((count, atom_count, 8, points), f32),
        ),
        in_specs=[any_spec] * 3,
        out_specs=(any_spec,) * 3,
        scratch_shapes=[
            pltpu.SemaphoreType.DMA((3,)),
            pltpu.SemaphoreType.DMA((count,)),
            pltpu.SemaphoreType.DMA((count,)),
        ]
        + [pltpu.SemaphoreType.DMA((2, size)) for size in (dom_y, dom_x, bands) for _ in range(2)],
        compiler_params=pltpu.CompilerParams(collective_id=0, has_side_effects=True),
    )(orbitals, local_potential, pack)

    along = np.zeros((nz, nz), np.float32)
    for i in range(nz):
        for j in range(max(0, i - reach), min(nz, i + reach + 1)):
            along[i, j] = scale * stencil[abs(i - j)] * (3.0 if i == j else 1.0)

    field_shape = (nx + 2 * reach, ny + 2 * pad_y + 8, nz)
    filt, image = pl.pallas_call(
        functools.partial(compute_kernel, (count, atom_count, proj_count, dom_y, size_x, size_y)),
        out_shape=(jax.ShapeDtypeStruct((nx, ny, nz), f32),) * 2,
        in_specs=[any_spec] * 3 + [vmem],
        out_specs=(any_spec, any_spec),
        scratch_shapes=[
            pltpu.VMEM((atoms, proj_count, box, box_y, nz), f32),
            pltpu.VMEM(field_shape, f32),
            pltpu.VMEM(field_shape, f32),
            pltpu.VMEM((atoms, proj_count, nz), f32),
            pltpu.VMEM((atoms, proj_count, nz), f32),
            pltpu.VMEM((nx, ny, nz), f32),
            pltpu.VMEM((nx, ny, nz), f32),
            pltpu.VMEM(packs.shape, f32),
            pltpu.SMEM((count, atom_count, 128), f32),
            pltpu.SemaphoreType.DMA((7,)),
        ],
        compiler_params=pltpu.CompilerParams(vmem_limit_bytes=48 << 20),
    )(whole_orb.reshape(nx, ny, nz), whole_pot.reshape(nx, ny, nz), packs, jnp.asarray(along))

    orbs = orb_count * bands
    half = size_x // bands
    rows = half * size_y
    shape = (dom_x, bands, half, dom_y, size_y, nz)
    sem = pltpu.SemaphoreType.DMA
    new, res, sub = pl.pallas_call(
        functools.partial(project_kernel, (dom_x, dom_y, bands, float(nx * ny * nz))),
        out_shape=(
            jax.ShapeDtypeStruct((orb_count, bands, half, size_y, nz), f32),
            jax.ShapeDtypeStruct((orb_count, bands, half, size_y, nz), f32),
            jax.ShapeDtypeStruct((orbs, orbs), f32),
        ),
        in_specs=[any_spec] * 2,
        out_specs=(any_spec, any_spec, vmem),
        scratch_shapes=[
            pltpu.VMEM((2 * orbs, half, size_y, nz), f32),
            pltpu.VMEM((2 * orbs, half, size_y, nz), f32),
            pltpu.VMEM((2, dom_x * bands, orbs, orbs), f32),
            pltpu.VMEM((2, dom_y, orbs, orbs), f32),
            sem((2,)),
            sem((2, orbs)),
            sem((2, orbs)),
            sem((2, dom_x * bands)),
            sem((2, dom_x * bands)),
            sem((2, dom_y)),
            sem((2, dom_y)),
            sem((2,)),
            sem((2, bands)),
            sem((2, bands)),
        ],
        compiler_params=pltpu.CompilerParams(
            collective_id=1, has_side_effects=True, vmem_limit_bytes=32 << 20
        ),
    )(filt.reshape(shape), image.reshape(shape))
    return (new.reshape(orbitals.shape), res.reshape(orbitals.shape), sub)


def per_device(orbitals, local_potential, atom_cell, support_offset, projector, coupling):
    domains = lax.axis_size("gx") * lax.axis_size("gy")
    bands = lax.axis_size("band")
    if orbitals.shape[0] == domains and orbitals.shape[1] % bands == 0 and atom_cell.shape[2] == bands:
        plan = per_device_whole
    else:
        plan = per_device_halo
    return plan(orbitals, local_potential, atom_cell, support_offset, projector, coupling)


def solution(mesh):
    in_specs = (
        P("band", "gx", "gy", None),
        P("gx", "gy", None),
        P("gx", "gy", None),
        P(None, "gx", "gy", None, None),
        P("gx", "gy", None, None, None),
        P("gx", "gy", None, None),
    )
    out_specs = (P("band", "gx", "gy", None), P("band", "gx", "gy", None), P())
    return jax.shard_map(
        per_device, mesh=mesh, in_specs=in_specs, out_specs=out_specs, check_vma=False
    )
```

```python
import functools

import jax
import jax.numpy as jnp
import numpy as np
from jax import lax
from jax.experimental import pallas as pl
from jax.experimental.pallas import tpu as pltpu
from jax.sharding import PartitionSpec as P

spacing = 0.4
low_edge = 6.0
top_edge = 150.0
stencil = (
    -5369.0 / 1800.0,
    12.0 / 7.0,
    -15.0 / 56.0,
    10.0 / 189.0,
    -1.0 / 112.0,
    2.0 / 1925.0,
    -1.0 / 16632.0,
)
highest = lax.Precision.HIGHEST


def with_halo(cells, sides, width):
    for axis, dim in sides:
        count = lax.axis_size(axis)
        ends = count - 1
        head = lax.slice_in_dim(cells, 0, width, axis=dim)
        tail = lax.slice_in_dim(cells, cells.shape[dim] - width, cells.shape[dim], axis=dim)
        cells = jnp.concatenate(
            [
                lax.ppermute(tail, axis, [(i, (i + 1) % count) for i in range(ends)]),
                cells,
                lax.ppermute(head, axis, [((i + 1) % count, i) for i in range(ends)]),
            ],
            axis=dim,
        )
    return cells


def kinetic_part(extended, orbital_block):
    size_x, size_y, size_z = (
        orbital_block.shape[1],
        orbital_block.shape[2],
        orbital_block.shape[3],
    )
    padded_z = jnp.pad(orbital_block, ((0, 0), (0, 0), (0, 0), (6, 6)))
    summed = 3.0 * stencil[0] * orbital_block
    for stride in range(1, 7):
        along_x = (
            extended[:, 6 + stride : 6 + stride + size_x, 6 : 6 + size_y]
            + extended[:, 6 - stride : 6 - stride + size_x, 6 : 6 + size_y]
        )
        along_y = (
            extended[:, 6 : 6 + size_x, 6 + stride : 6 + stride + size_y]
            + extended[:, 6 : 6 + size_x, 6 - stride : 6 - stride + size_y]
        )
        along_z = (
            padded_z[..., 6 + stride : 6 + stride + size_z]
            + padded_z[..., 6 - stride : 6 - stride + size_z]
        )
        summed = summed + stencil[stride] * (along_x + along_y + along_z)
    return -0.5 / spacing**2 * summed


def prepare_tables(atom_cell, support_offset, projector, size_x, size_y, size_z):
    home_cell = atom_cell[..., None]
    relative = jnp.stack(
        [
            home_cell // (size_y * size_z) + support_offset[0],
            home_cell // size_z % size_y + support_offset[1],
            home_cell % size_z + support_offset[2],
        ]
    )
    rel_near = with_halo(relative, (("gx", 1), ("gy", 2)), 1)
    beta_near = with_halo(projector, (("gx", 0), ("gy", 1)), 1)
    atom_count, proj_count = (projector.shape[2], projector.shape[3])
    cell_count = size_x * size_y * size_z
    frame_x = (lax.broadcasted_iota(jnp.int32, (3, 3, 1, 1), 0) - 1) * size_x
    frame_y = (lax.broadcasted_iota(jnp.int32, (3, 3, 1, 1), 1) - 1) * size_y
    coord_x = rel_near[0] + frame_x
    coord_y = rel_near[1] + frame_y
    coord_z = rel_near[2]
    inside = (
        (coord_x >= 0)
        & (coord_x < size_x)
        & (coord_y >= 0)
        & (coord_y < size_y)
        & (coord_z >= 0)
        & (coord_z < size_z)
    ).astype(jnp.float32)
    cell_index = (
        jnp.clip(coord_x, 0, size_x - 1) * size_y + jnp.clip(coord_y, 0, size_y - 1)
    ) * size_z + jnp.clip(coord_z, 0, size_z - 1)
    near_columns = jnp.arange(9 * atom_count * proj_count, dtype=jnp.int32).reshape(
        3, 3, atom_count, proj_count, 1
    )
    near_flat = near_columns * cell_count + cell_index[:, :, :, None, :]
    near_values = beta_near * inside[:, :, :, None, :]
    table_near = (
        jnp.zeros((9 * atom_count * proj_count * cell_count,), jnp.float32)
        .at[near_flat.reshape(-1)]
        .add(near_values.reshape(-1))
    )
    table_near = table_near.reshape(3, 3, atom_count, proj_count, cell_count)
    own_rel = relative[:, 0, 0]
    own_x = own_rel[0] + 6
    own_y = own_rel[1] + 6
    own_z = own_rel[2]
    own_zin = ((own_z >= 0) & (own_z < size_z)).astype(jnp.float32)
    own_index = (own_x * (size_y + 12) + own_y) * size_z + jnp.clip(own_z, 0, size_z - 1)
    ext_count = (size_x + 12) * (size_y + 12) * size_z
    own_columns = jnp.arange(atom_count * proj_count, dtype=jnp.int32).reshape(
        atom_count, proj_count, 1
    )
    own_flat = own_columns * ext_count + own_index[:, None, :]
    own_values = projector[0, 0] * own_zin[:, None, :]
    table_own = (
        jnp.zeros((atom_count * proj_count * ext_count,), jnp.float32)
        .at[own_flat.reshape(-1)]
        .add(own_values.reshape(-1))
    )
    table_own = table_own.reshape(atom_count, proj_count, ext_count)
    return (table_near, table_own)


def apply_hamiltonian(orbital_block, local_potential, tables, coupling_own):
    table_near, table_own = tables
    orb_count = orbital_block.shape[0]
    atom_count, proj_count = coupling_own.shape
    flat_block = orbital_block.reshape(orb_count, -1)
    extended = with_halo(orbital_block, (("gx", 1), ("gy", 2)), 6)
    kinetic = kinetic_part(extended, orbital_block)
    partial_terms = jnp.einsum("ijanc,bc->ijanb", table_near, flat_block, precision=highest)
    received = with_halo(partial_terms.reshape(1, 1, -1), (("gx", 0), ("gy", 1)), 1)
    grouped = received.reshape(3, 3, 3, 3, atom_count, proj_count, orb_count)
    coefficients = grouped[1, 1, 1, 1]
    for row_pos in range(3):
        for col_pos in range(3):
            if row_pos != 1 or col_pos != 1:
                coefficients = coefficients + grouped[row_pos, col_pos, 2 - row_pos, 2 - col_pos]
    scaled = coupling_own[:, :, None] * coefficients
    near_coefs = with_halo(scaled.reshape(1, 1, -1), (("gx", 0), ("gy", 1)), 1)
    near_coefs = near_coefs.reshape(3, 3, atom_count, proj_count, orb_count)
    projector_term = jnp.einsum("ijanc,ijanb->bc", table_near, near_coefs, precision=highest)
    return kinetic + local_potential * orbital_block + projector_term.reshape(orbital_block.shape)


def inverse_factor(intersection):
    factor = jnp.linalg.cholesky(intersection)
    identity = jnp.eye(intersection.shape[0], dtype=jnp.float32)
    return lax.linalg.triangular_solve(factor, identity, left_side=True, lower=True)


def per_device_halo(orbitals, local_potential, atom_cell, support_offset, projector, coupling):
    orb_count, size_x, size_y, size_z = orbitals.shape
    tables = prepare_tables(atom_cell, support_offset, projector, size_x, size_y, size_z)
    coupling_own = coupling[0, 0]

    def hamiltonian(orbital_block):
        return apply_hamiltonian(orbital_block, local_potential, tables, coupling_own)

    middle = 0.5 * (top_edge + low_edge)
    half_width = 0.5 * (top_edge - low_edge)
    total_cells = float(size_x * size_y * size_z * lax.axis_size("gx") * lax.axis_size("gy"))
    band_start = lax.axis_index("band") * orb_count
    first_term = (hamiltonian(orbitals) - middle * orbitals) / half_width
    filtered = 2.0 * (hamiltonian(first_term) - middle * first_term) / half_width - orbitals
    filt_flat = filtered.reshape(orb_count, -1)
    orbs_all = orb_count * lax.axis_size("band")
    empty_square = jnp.zeros((orbs_all, orbs_all), jnp.float32)
    whole_block = lax.all_gather(filt_flat, "band", axis=0, tiled=True)
    over_cols = jnp.einsum("kc,lc->kl", whole_block, filt_flat, precision=highest) / total_cells
    intersection = lax.psum(
        lax.dynamic_update_slice(empty_square, over_cols, (0, band_start)), ("gx", "gy", "band")
    )
    inverse = inverse_factor(intersection)
    rotated_all = jnp.dot(inverse, whole_block, precision=highest)
    rotated = lax.dynamic_slice_in_dim(rotated_all, band_start, orb_count, 0)
    image_own = hamiltonian(rotated.reshape(orbitals.shape)).reshape(orb_count, -1)
    sub_cols = jnp.einsum("kc,lc->kl", rotated_all, image_own, precision=highest) / total_cells
    subspace = lax.psum(
        lax.dynamic_update_slice(empty_square, sub_cols, (0, band_start)), ("gx", "gy", "band")
    )
    cols_own = lax.dynamic_slice_in_dim(subspace, band_start, orb_count, 1)
    residual = (
        image_own - jnp.einsum("kl,kc->lc", cols_own, rotated_all, precision=highest)
    ) / half_width
    return (rotated.reshape(orbitals.shape), residual.reshape(orbitals.shape), subspace)


MESH = pl.DeviceIdType.MESH
reach = 6
box = 2 * reach + 1
box_y = 16
pad_y = 8
scale = -0.5 / spacing**2


def gather_kernel(
    dims, orb_ref, pot_ref, pack_ref, orb_out, pot_out, pack_out, local_sem, send_sem, recv_sem, *stage_sems
):
    dom_x, dom_y, bands = dims
    count = dom_x * dom_y
    my_x, my_y, my_band = lax.axis_index("gx"), lax.axis_index("gy"), lax.axis_index("band")
    me = my_x * dom_y + my_y
    half = pot_ref.shape[0] // bands
    mine = pl.ds(my_band * half, half)

    barrier = pltpu.get_barrier_semaphore()

    def greet(step, carry):
        peer = lax.rem(me + step, count)
        pl.semaphore_signal(
            barrier, inc=1, device_id={"gx": peer // dom_y, "gy": lax.rem(peer, dom_y)}, device_id_type=MESH
        )
        return carry

    lax.fori_loop(1, count, greet, 0)
    for step in range(1, bands):
        pl.semaphore_signal(
            barrier, inc=1, device_id={"band": lax.rem(my_band + step, bands)}, device_id_type=MESH
        )

    def orb_copy(peer, source):
        return pltpu.make_async_remote_copy(
            src_ref=orb_ref.at[peer],
            dst_ref=orb_out.at[source // dom_y, :, lax.rem(source, dom_y)],
            send_sem=send_sem.at[peer],
            recv_sem=recv_sem.at[source],
            device_id={"gx": peer // dom_y, "gy": lax.rem(peer, dom_y)},
            device_id_type=MESH,
        )

    def stage_copies(stage, axis, peer, source):
        if stage == 0:
            pairs = (
                (pack_ref.at[my_band], pack_out.at[my_x * dom_y + source, my_band]),
                (pot_ref.at[mine], pot_out.at[my_x, mine, source]),
            )
        elif stage == 1:
            block = pack_out.at[pl.ds(source * dom_y, dom_y), my_band]
            strip = pot_out.at[source, mine]
            pairs = ((block, block), (strip, strip))
        else:
            block = pack_out.at[:, source]
            strip = pot_out.at[:, pl.ds(source * half, half)]
            pairs = ((block, block), (strip, strip))
        return [
            pltpu.make_async_remote_copy(
                src_ref=src,
                dst_ref=dst,
                send_sem=stage_sems[2 * stage].at[kind, peer],
                recv_sem=stage_sems[2 * stage + 1].at[kind, source],
                device_id={axis: peer},
                device_id_type=MESH,
            )
            for kind, (src, dst) in enumerate(pairs)
        ]

    def start_stage(stage, axis, place, size):
        for step in range(1, size):
            for copy in stage_copies(stage, axis, lax.rem(place + step, size), place):
                copy.start()

    def end_stage(stage, axis, place, size):
        for step in range(1, size):
            peer = lax.rem(place + step, size)
            for copy in stage_copies(stage, axis, peer, place):
                copy.wait_send()
            for copy in stage_copies(stage, axis, peer, peer):
                copy.wait_recv()

    own = [
        pltpu.make_async_copy(pack_ref.at[my_band], pack_out.at[me, my_band], local_sem.at[0]),
        pltpu.make_async_copy(pot_ref.at[mine], pot_out.at[my_x, mine, my_y], local_sem.at[1]),
        pltpu.make_async_copy(orb_ref.at[me], orb_out.at[my_x, :, my_y], local_sem.at[2]),
    ]
    for copy in own:
        copy.start()
    pl.semaphore_wait(barrier, count - 1 + bands - 1)

    def send(step, carry):
        orb_copy(lax.rem(me + step, count), me).start()
        return carry

    def finish(step, carry):
        peer = lax.rem(me + step, count)
        orb_copy(peer, me).wait_send()
        orb_copy(peer, peer).wait_recv()
        return carry

    early = count // 4
    start_stage(0, "gy", my_y, dom_y)
    lax.fori_loop(1, early, send, 0)
    end_stage(0, "gy", my_y, dom_y)
    own[0].wait()
    own[1].wait()
    start_stage(1, "gx", my_x, dom_x)
    lax.fori_loop(early, count, send, 0)
    end_stage(1, "gx", my_x, dom_x)
    start_stage(2, "band", my_band, bands)
    end_stage(2, "band", my_band, bands)
    lax.fori_loop(1, count, finish, 0)
    own[2].wait()


def compute_kernel(
    dims,
    orb_any,
    pot_any,
    pack_any,
    along_ref,
    filt_any,
    image_any,
    table,
    field,
    out,
    sums,
    coefs,
    orb_ref,
    pot_ref,
    pack_ref,
    small,
    copy_sem,
):
    count, atom_count, proj_count, dom_y, size_x, size_y = dims
    nx, ny, nz = orb_ref.shape
    points = pack_ref.shape[3]
    fetch_pack = pltpu.make_async_copy(pack_any, pack_ref, copy_sem.at[0])
    fetch_small = pltpu.make_async_copy(pack_any.at[:, :, proj_count + 1, pl.ds(0, 128)], small, copy_sem.at[1])
    fetch_pack.start()
    fetch_small.start()
    field[...] = jnp.zeros_like(field)
    inside_field = field.at[pl.ds(reach, nx), pl.ds(pad_y, ny), :]
    fetch_field = pltpu.make_async_copy(orb_any, inside_field, copy_sem.at[2])
    fetch_pot = pltpu.make_async_copy(pot_any, pot_ref, copy_sem.at[3])
    fetch_orb = pltpu.make_async_copy(orb_any, orb_ref, copy_sem.at[4])
    fetch_field.start()
    fetch_pot.start()
    fetch_orb.start()

    def home_of(dom, atom):
        cell = small[dom, atom, proj_count].astype(jnp.int32)
        home_x = dom // dom_y * size_x + cell // (size_y * nz)
        home_y = lax.rem(dom, dom_y) * size_y + lax.rem(cell // nz, size_y) + pad_y - reach
        return home_x, home_y, lax.rem(cell, nz)

    rows = box * box_y
    wide = 16
    lane = lax.broadcasted_iota(jnp.int32, (rows, nz), 1)
    row_xy = lax.broadcasted_iota(jnp.int32, (rows, points), 0)
    row_z = lax.broadcasted_iota(jnp.int32, (wide, points), 0)

    def build(dom, carry):
        for atom in range(atom_count):
            cell = pack_ref[dom, atom, proj_count : proj_count + 1, :].astype(jnp.int32)
            hot_xy = jnp.where(row_xy == lax.shift_right_arithmetic(cell, 4), 1.0, 0.0).astype(jnp.bfloat16)
            hot_z = row_z == (cell & 15)
            values = jnp.concatenate(
                [
                    jnp.where(hot_z, pack_ref[dom, atom, n : n + 1, :], 0.0)
                    for n in range(proj_count)
                ],
                axis=0,
            )
            high = values.astype(jnp.bfloat16)
            low = (values - high.astype(jnp.float32)).astype(jnp.bfloat16)
            both = jnp.concatenate([high, low], axis=0)
            boxes = lax.dot_general(hot_xy, both, (((1,), (1,)), ((), ())), preferred_element_type=jnp.float32)
            boxes = boxes + pltpu.roll(boxes, proj_count * wide, 1)
            at = dom * atom_count + atom
            low_z = home_of(dom, atom)[2] - reach
            for n in range(proj_count):
                kept = jnp.where((lane >= n * wide) & (lane < (n + 1) * wide), boxes, 0.0)
                moved = pltpu.roll(kept, lax.rem(low_z - n * wide + 2 * nz, nz), 1)
                table[at, n] = moved.reshape(box, box_y, nz)
        return carry

    out[...] = jnp.zeros_like(out)
    inner = pl.ds(pad_y, ny)
    fetch_pack.wait()
    fetch_small.wait()
    lax.fori_loop(0, count, build, 0, unroll=2)
    fetch_field.wait()
    fetch_pot.wait()
    fetch_orb.wait()

    def hamiltonian():
        def project(at, carry):
            x0, y0, _ = home_of(at // atom_count, lax.rem(at, atom_count))
            totals = [jnp.zeros((box_y, nz), jnp.float32) for _ in range(proj_count)]
            for dx in range(box):
                part = field[x0 + dx, pl.ds(y0, box_y), :]
                for n in range(proj_count):
                    totals[n] = totals[n] + table[at, n, dx] * part
            stacked = [jnp.sum(total, axis=0, keepdims=True) for total in totals]
            sums[at] = jnp.concatenate(stacked, axis=0)
            return carry

        lax.fori_loop(0, count * atom_count, project, 0, unroll=2)
        scaled = jnp.sum(sums[...], axis=2, keepdims=True)
        coefs[...] = jnp.broadcast_to(scaled, coefs.shape)

        chunk = 8
        for start in range(0, nx, chunk):
            block = field[reach + start : reach + start + chunk, pad_y : pad_y + ny, :]
            z_part = jnp.dot(
                block.reshape(chunk * ny, nz), along_ref[...], precision=highest, preferred_element_type=jnp.float32
            )
            out[reach + start : reach + start + chunk, pad_y : pad_y + ny, :] = z_part.reshape(chunk, ny, nz)

        def stencil_row(row, carry):
            at = row + reach
            summed = out[at, inner, :] + pot_ref[row] * field[at, inner, :]
            for k in range(1, reach + 1):
                around = (
                    field[at + k, inner, :]
                    + field[at - k, inner, :]
                    + field[at, pl.ds(pad_y + k, ny), :]
                    + field[at, pl.ds(pad_y - k, ny), :]
                )
                summed = summed + (scale * stencil[k]) * around
            out[at, inner, :] = summed
            return carry

        lax.fori_loop(0, nx, stencil_row, 0, unroll=2)

        def spread(at, carry):
            x0, y0, _ = home_of(at // atom_count, lax.rem(at, atom_count))
            weights = [
                jnp.broadcast_to(
                    coefs[at, n : n + 1, :] * small[at // atom_count, lax.rem(at, atom_count), n], (box_y, nz)
                )
                for n in range(proj_count)
            ]
            for dx in range(box):
                added = out[x0 + dx, pl.ds(y0, box_y), :]
                for n in range(proj_count):
                    added = added + table[at, n, dx] * weights[n]
                out[x0 + dx, pl.ds(y0, box_y), :] = added
            return carry

        lax.fori_loop(0, count * atom_count, spread, 0)

    middle = 0.5 * (top_edge + low_edge)
    half_width = 0.5 * (top_edge - low_edge)
    hamiltonian()

    def first_row(row, carry):
        at = row + reach
        field[at, inner, :] = (out[at, inner, :] - middle * field[at, inner, :]) * (1.0 / half_width)
        return carry

    lax.fori_loop(0, nx, first_row, 0)
    hamiltonian()

    def filter_row(row, carry):
        at = row + reach
        value = (out[at, inner, :] - middle * field[at, inner, :]) * (2.0 / half_width) - orb_ref[row]
        field[at, inner, :] = value
        orb_ref[row] = value
        return carry

    lax.fori_loop(0, nx, filter_row, 0)
    store_filt = pltpu.make_async_copy(orb_ref, filt_any, copy_sem.at[5])
    store_filt.start()
    hamiltonian()
    store_image = pltpu.make_async_copy(out.at[pl.ds(reach, nx), pl.ds(pad_y, ny), :], image_any, copy_sem.at[6])
    store_image.start()
    store_filt.wait()
    store_image.wait()


def project_kernel(
    dims,
    filt_ref,
    image_ref,
    new_out,
    res_out,
    sub_out,
    cells,
    result,
    plane,
    column,
    local_sem,
    send_sem,
    recv_sem,
    plane_send,
    plane_recv,
    column_send,
    column_recv,
    out_sem,
    pair_send,
    pair_recv,
):
    dom_x, dom_y, bands, total_cells = dims
    per_band = dom_x * dom_y
    orbs = per_band * bands
    my_x, my_y, my_band = lax.axis_index("gx"), lax.axis_index("gy"), lax.axis_index("band")
    me = my_band * per_band + my_x * dom_y + my_y
    rows = cells.shape[1] * cells.shape[2]

    def place(peer):
        inside = lax.rem(peer, per_band)
        return {"gx": inside // dom_y, "gy": lax.rem(inside, dom_y), "band": peer // per_band}

    barrier = pltpu.get_barrier_semaphore()

    def greet(step, carry):
        pl.semaphore_signal(barrier, inc=1, device_id=place(lax.rem(me + step, orbs)), device_id_type=MESH)
        return carry

    lax.fori_loop(1, orbs, greet, 0)

    def chunk_of(ref, peer):
        inside = lax.rem(peer, per_band)
        return ref.at[inside // dom_y, peer // per_band, :, lax.rem(inside, dom_y)]

    def parts(peer, source):
        return [
            pltpu.make_async_remote_copy(
                src_ref=chunk_of(ref, peer),
                dst_ref=cells.at[kind * orbs + source],
                send_sem=send_sem.at[kind, peer],
                recv_sem=recv_sem.at[kind, source],
                device_id=place(peer),
                device_id_type=MESH,
            )
            for kind, ref in enumerate((filt_ref, image_ref))
        ]

    own = [
        pltpu.make_async_copy(chunk_of(ref, me), cells.at[kind * orbs + me], local_sem.at[kind])
        for kind, ref in enumerate((filt_ref, image_ref))
    ]
    for copy in own:
        copy.start()
    pl.semaphore_wait(barrier, orbs - 1)

    for kind in range(2):

        def send(step, carry, kind=kind):
            parts(lax.rem(me + step, orbs), me)[kind].start()
            return carry

        lax.fori_loop(1, orbs, send, 0)

    def finish(kind):
        def one(step, carry):
            peer = lax.rem(me + step, orbs)
            parts(peer, me)[kind].wait_send()
            parts(peer, peer)[kind].wait_recv()
            return carry

        lax.fori_loop(1, orbs, one, 0)
        own[kind].wait()

    flat = cells.reshape(2 * orbs * rows, cells.shape[3])
    flat_result = result.reshape(2 * orbs * rows, cells.shape[3])

    def product(left, right, dims_in):
        return lax.dot_general(left, right, (dims_in, ((), ())), precision=highest, preferred_element_type=jnp.float32)

    def load(ref, kind, row):
        return ref[pl.ds(kind * orbs * rows + row, orbs, stride=rows), :]

    in_plane = dom_x * bands
    my_plane = my_x * bands + my_band

    def plane_copy(peer, slot):
        return pltpu.make_async_remote_copy(
            src_ref=plane.at[my_plane],
            dst_ref=plane.at[slot],
            send_sem=plane_send.at[peer],
            recv_sem=plane_recv.at[slot],
            device_id={"gx": peer // bands, "gy": my_y, "band": lax.rem(peer, bands)},
            device_id_type=MESH,
        )

    def column_copy(peer, slot):
        return pltpu.make_async_remote_copy(
            src_ref=column.at[my_y],
            dst_ref=column.at[slot],
            send_sem=column_send.at[peer],
            recv_sem=column_recv.at[slot],
            device_id={"gx": my_x, "gy": peer, "band": my_band},
            device_id_type=MESH,
        )

    def summed(share, box_ref, copy_of, place_at, size):
        box_ref[place_at] = share
        for step in range(1, size):
            copy_of(lax.rem(place_at + step, size), place_at).start()
        for step in range(1, size):
            peer = lax.rem(place_at + step, size)
            copy_of(peer, place_at).wait_send()
            copy_of(peer, peer).wait_recv()
        total = box_ref[0]
        for slot in range(1, size):
            total = total + box_ref[slot]
        return total

    def all_sum(share):
        share = summed(share, plane, plane_copy, my_plane, in_plane)
        return summed(share, column, column_copy, my_y, dom_y) * (1.0 / total_cells)

    sums_across = plane.shape[1] // 2
    groups = orbs // sums_across

    def dense(square):
        return jnp.concatenate([square[g * sums_across : (g + 1) * sums_across] for g in range(groups)], axis=1)

    def square_of(packed):
        return jnp.concatenate([packed[:, g * orbs : (g + 1) * orbs] for g in range(groups)], axis=0)

    finish(0)
    gram = jnp.zeros((orbs, orbs), jnp.float32)
    for row in range(rows):
        part = load(flat, 0, row)
        gram = gram + product(part, part, ((1,), (1,)))
    finish(1)
    mixed_gram = jnp.zeros((orbs, orbs), jnp.float32)
    for row in range(rows):
        mixed_gram = mixed_gram + product(load(flat, 0, row), load(flat, 1, row), ((1,), (1,)))
    totals = all_sum(jnp.concatenate([dense(gram), dense(mixed_gram)], axis=0))
    total = square_of(totals[:sums_across])
    crossed = square_of(totals[sums_across:])

    row_at = lax.broadcasted_iota(jnp.int32, (orbs, orbs), 0)
    col_at = lax.broadcasted_iota(jnp.int32, (orbs, orbs), 1)
    eye = jnp.where(row_at == col_at, 1.0, 0.0)
    work = jnp.concatenate([total, eye], axis=1)
    row_wide = lax.broadcasted_iota(jnp.int32, (orbs, 2 * orbs), 0)
    for k in range(orbs):
        pivot_row = work[k : k + 1, :]
        pivot = work[k : k + 1, k : k + 1]
        factor = jnp.where(row_wide[:, :1] > k, work[:, k : k + 1] / pivot, 0.0)
        work = work - factor * pivot_row
    diagonal = jnp.sum(work[:, :orbs] * eye, axis=1, keepdims=True)
    inverse = work[:, orbs:] / jnp.sqrt(diagonal)

    outs = (new_out, res_out)

    def pair_copy(kind, other, half):
        return pltpu.make_async_remote_copy(
            src_ref=result.at[pl.ds(kind * orbs + other * per_band, per_band)],
            dst_ref=outs[kind].at[:, half],
            send_sem=pair_send.at[kind, other],
            recv_sem=pair_recv.at[kind, half],
            device_id={"gx": my_x, "gy": my_y, "band": other},
            device_id_type=MESH,
        )

    def keep(kind):
        source = result.at[pl.ds(kind * orbs + my_band * per_band, per_band)]
        return pltpu.make_async_copy(source, outs[kind].at[:, my_band], out_sem.at[kind])

    def give(kind):
        for step in range(1, bands):
            pair_copy(kind, lax.rem(my_band + step, bands), my_band).start()
        keep(kind).start()

    for row in range(rows):
        flat_result[pl.ds(row, orbs, stride=rows), :] = product(inverse, load(flat, 0, row), ((1,), (0,)))
    give(0)

    projected = product(inverse, crossed, ((1,), (0,)))
    subspace = product(projected, inverse, ((1,), (1,)))
    sub_out[...] = subspace
    half_width = 0.5 * (top_edge - low_edge)
    mixed = product(subspace, inverse, ((0,), (0,))) * (-1.0 / half_width)
    rotation = jnp.concatenate([mixed, inverse * (1.0 / half_width)], axis=1)
    for row in range(rows):
        both = jnp.concatenate([load(flat, 0, row), load(flat, 1, row)], axis=0)
        flat_result[pl.ds(orbs * rows + row, orbs, stride=rows), :] = product(rotation, both, ((1,), (0,)))
    give(1)

    for kind in range(2):
        for step in range(1, bands):
            other = lax.rem(my_band + step, bands)
            pair_copy(kind, other, my_band).wait_send()
            pair_copy(kind, other, other).wait_recv()
        keep(kind).wait()


def per_device_whole(orbitals, local_potential, atom_cell, support_offset, projector, coupling):
    orb_count, size_x, size_y, nz = orbitals.shape
    dom_x, dom_y, bands = lax.axis_size("gx"), lax.axis_size("gy"), lax.axis_size("band")
    count = dom_x * dom_y
    nx, ny = dom_x * size_x, dom_y * size_y
    atom_count, proj_count, points = projector.shape[2:]
    atoms = count * atom_count
    any_spec = pl.BlockSpec(memory_space=pl.ANY)
    vmem = pl.BlockSpec(memory_space=pltpu.VMEM)

    cell = atom_cell[0, 0]
    offset = support_offset[:, 0, 0]
    home_z = cell % nz
    point_z = home_z[:, None] + offset[2]
    box_cell = ((offset[0] + reach) * box_y + offset[1] + reach) * 16 + offset[2] + reach
    box_cell = jnp.where((point_z >= 0) & (point_z < nz), box_cell, -1).astype(jnp.float32)
    small = jnp.concatenate([coupling[0, 0], cell[:, None].astype(jnp.float32)], axis=1)
    pack = jnp.concatenate(
        [
            projector[0, 0],
            box_cell[:, None],
            jnp.pad(small, ((0, 0), (0, points - small.shape[1])))[:, None],
            jnp.zeros((atom_count, 8 - proj_count - 2, points), jnp.float32),
        ],
        axis=1,
    )
    f32 = jnp.float32
    whole_orb, whole_pot, packs = pl.pallas_call(
        functools.partial(gather_kernel, (dom_x, dom_y, bands)),
        out_shape=(
            jax.ShapeDtypeStruct((dom_x, size_x, dom_y, size_y, nz), f32),
            jax.ShapeDtypeStruct((dom_x, size_x, dom_y, size_y, nz), f32),
            jax.ShapeDtypeStruct((count, atom_count, 8, points), f32),
        ),
        in_specs=[any_spec] * 3,
        out_specs=(any_spec,) * 3,
        scratch_shapes=[
            pltpu.SemaphoreType.DMA((3,)),
            pltpu.SemaphoreType.DMA((count,)),
            pltpu.SemaphoreType.DMA((count,)),
        ]
        + [pltpu.SemaphoreType.DMA((2, size)) for size in (dom_y, dom_x, bands) for _ in range(2)],
        compiler_params=pltpu.CompilerParams(collective_id=0, has_side_effects=True),
    )(orbitals, local_potential, pack)

    along = np.zeros((nz, nz), np.float32)
    for i in range(nz):
        for j in range(max(0, i - reach), min(nz, i + reach + 1)):
            along[i, j] = scale * stencil[abs(i - j)] * (3.0 if i == j else 1.0)

    field_shape = (nx + 2 * reach, ny + 2 * pad_y + 8, nz)
    filt, image = pl.pallas_call(
        functools.partial(compute_kernel, (count, atom_count, proj_count, dom_y, size_x, size_y)),
        out_shape=(jax.ShapeDtypeStruct((nx, ny, nz), f32),) * 2,
        in_specs=[any_spec] * 3 + [vmem],
        out_specs=(any_spec, any_spec),
        scratch_shapes=[
            pltpu.VMEM((atoms, proj_count, box, box_y, nz), f32),
            pltpu.VMEM(field_shape, f32),
            pltpu.VMEM(field_shape, f32),
            pltpu.VMEM((atoms, proj_count, nz), f32),
            pltpu.VMEM((atoms, proj_count, nz), f32),
            pltpu.VMEM((nx, ny, nz), f32),
            pltpu.VMEM((nx, ny, nz), f32),
            pltpu.VMEM(packs.shape, f32),
            pltpu.SMEM((count, atom_count, 128), f32),
            pltpu.SemaphoreType.DMA((7,)),
        ],
        compiler_params=pltpu.CompilerParams(vmem_limit_bytes=48 << 20),
    )(whole_orb.reshape(nx, ny, nz), whole_pot.reshape(nx, ny, nz), packs, jnp.asarray(along))

    orbs = orb_count * bands
    sum_rows = orbs // max(1, nz // orbs)
    half = size_x // bands
    rows = half * size_y
    shape = (dom_x, bands, half, dom_y, size_y, nz)
    sem = pltpu.SemaphoreType.DMA
    new, res, sub = pl.pallas_call(
        functools.partial(project_kernel, (dom_x, dom_y, bands, float(nx * ny * nz))),
        out_shape=(
            jax.ShapeDtypeStruct((orb_count, bands, half, size_y, nz), f32),
            jax.ShapeDtypeStruct((orb_count, bands, half, size_y, nz), f32),
            jax.ShapeDtypeStruct((orbs, orbs), f32),
        ),
        in_specs=[any_spec] * 2,
        out_specs=(any_spec, any_spec, vmem),
        scratch_shapes=[
            pltpu.VMEM((2 * orbs, half, size_y, nz), f32),
            pltpu.VMEM((2 * orbs, half, size_y, nz), f32),
            pltpu.VMEM((dom_x * bands, 2 * sum_rows, orbs * orbs // sum_rows), f32),
            pltpu.VMEM((dom_y, 2 * sum_rows, orbs * orbs // sum_rows), f32),
            sem((2,)),
            sem((2, orbs)),
            sem((2, orbs)),
            sem((dom_x * bands,)),
            sem((dom_x * bands,)),
            sem((dom_y,)),
            sem((dom_y,)),
            sem((2,)),
            sem((2, bands)),
            sem((2, bands)),
        ],
        compiler_params=pltpu.CompilerParams(
            collective_id=1, has_side_effects=True, vmem_limit_bytes=32 << 20
        ),
    )(filt.reshape(shape), image.reshape(shape))
    return (new.reshape(orbitals.shape), res.reshape(orbitals.shape), sub)


def per_device(orbitals, local_potential, atom_cell, support_offset, projector, coupling):
    domains = lax.axis_size("gx") * lax.axis_size("gy")
    bands = lax.axis_size("band")
    if orbitals.shape[0] == domains and orbitals.shape[1] % bands == 0 and atom_cell.shape[2] == bands:
        plan = per_device_whole
    else:
        plan = per_device_halo
    return plan(orbitals, local_potential, atom_cell, support_offset, projector, coupling)


def solution(mesh):
    in_specs = (
        P("band", "gx", "gy", None),
        P("gx", "gy", None),
        P("gx", "gy", None),
        P(None, "gx", "gy", None, None),
        P("gx", "gy", None, None, None),
        P("gx", "gy", None, None),
    )
    out_specs = (P("band", "gx", "gy", None), P("band", "gx", "gy", None), P())
    return jax.shard_map(
        per_device, mesh=mesh, in_specs=in_specs, out_specs=out_specs, check_vma=False
    )
```

```python
import functools

import jax
import jax.numpy as jnp
import numpy as np
from jax import lax
from jax.experimental import pallas as pl
from jax.experimental.pallas import tpu as pltpu
from jax.sharding import PartitionSpec as P

spacing = 0.4
low_edge = 6.0
top_edge = 150.0
stencil = (
    -5369.0 / 1800.0,
    12.0 / 7.0,
    -15.0 / 56.0,
    10.0 / 189.0,
    -1.0 / 112.0,
    2.0 / 1925.0,
    -1.0 / 16632.0,
)
highest = lax.Precision.HIGHEST


def with_halo(cells, sides, width):
    for axis, dim in sides:
        count = lax.axis_size(axis)
        ends = count - 1
        head = lax.slice_in_dim(cells, 0, width, axis=dim)
        tail = lax.slice_in_dim(cells, cells.shape[dim] - width, cells.shape[dim], axis=dim)
        cells = jnp.concatenate(
            [
                lax.ppermute(tail, axis, [(i, (i + 1) % count) for i in range(ends)]),
                cells,
                lax.ppermute(head, axis, [((i + 1) % count, i) for i in range(ends)]),
            ],
            axis=dim,
        )
    return cells


def kinetic_part(extended, orbital_block):
    size_x, size_y, size_z = (
        orbital_block.shape[1],
        orbital_block.shape[2],
        orbital_block.shape[3],
    )
    padded_z = jnp.pad(orbital_block, ((0, 0), (0, 0), (0, 0), (6, 6)))
    summed = 3.0 * stencil[0] * orbital_block
    for stride in range(1, 7):
        along_x = (
            extended[:, 6 + stride : 6 + stride + size_x, 6 : 6 + size_y]
            + extended[:, 6 - stride : 6 - stride + size_x, 6 : 6 + size_y]
        )
        along_y = (
            extended[:, 6 : 6 + size_x, 6 + stride : 6 + stride + size_y]
            + extended[:, 6 : 6 + size_x, 6 - stride : 6 - stride + size_y]
        )
        along_z = (
            padded_z[..., 6 + stride : 6 + stride + size_z]
            + padded_z[..., 6 - stride : 6 - stride + size_z]
        )
        summed = summed + stencil[stride] * (along_x + along_y + along_z)
    return -0.5 / spacing**2 * summed


def prepare_tables(atom_cell, support_offset, projector, size_x, size_y, size_z):
    home_cell = atom_cell[..., None]
    relative = jnp.stack(
        [
            home_cell // (size_y * size_z) + support_offset[0],
            home_cell // size_z % size_y + support_offset[1],
            home_cell % size_z + support_offset[2],
        ]
    )
    rel_near = with_halo(relative, (("gx", 1), ("gy", 2)), 1)
    beta_near = with_halo(projector, (("gx", 0), ("gy", 1)), 1)
    atom_count, proj_count = (projector.shape[2], projector.shape[3])
    cell_count = size_x * size_y * size_z
    frame_x = (lax.broadcasted_iota(jnp.int32, (3, 3, 1, 1), 0) - 1) * size_x
    frame_y = (lax.broadcasted_iota(jnp.int32, (3, 3, 1, 1), 1) - 1) * size_y
    coord_x = rel_near[0] + frame_x
    coord_y = rel_near[1] + frame_y
    coord_z = rel_near[2]
    inside = (
        (coord_x >= 0)
        & (coord_x < size_x)
        & (coord_y >= 0)
        & (coord_y < size_y)
        & (coord_z >= 0)
        & (coord_z < size_z)
    ).astype(jnp.float32)
    cell_index = (
        jnp.clip(coord_x, 0, size_x - 1) * size_y + jnp.clip(coord_y, 0, size_y - 1)
    ) * size_z + jnp.clip(coord_z, 0, size_z - 1)
    near_columns = jnp.arange(9 * atom_count * proj_count, dtype=jnp.int32).reshape(
        3, 3, atom_count, proj_count, 1
    )
    near_flat = near_columns * cell_count + cell_index[:, :, :, None, :]
    near_values = beta_near * inside[:, :, :, None, :]
    table_near = (
        jnp.zeros((9 * atom_count * proj_count * cell_count,), jnp.float32)
        .at[near_flat.reshape(-1)]
        .add(near_values.reshape(-1))
    )
    table_near = table_near.reshape(3, 3, atom_count, proj_count, cell_count)
    own_rel = relative[:, 0, 0]
    own_x = own_rel[0] + 6
    own_y = own_rel[1] + 6
    own_z = own_rel[2]
    own_zin = ((own_z >= 0) & (own_z < size_z)).astype(jnp.float32)
    own_index = (own_x * (size_y + 12) + own_y) * size_z + jnp.clip(own_z, 0, size_z - 1)
    ext_count = (size_x + 12) * (size_y + 12) * size_z
    own_columns = jnp.arange(atom_count * proj_count, dtype=jnp.int32).reshape(
        atom_count, proj_count, 1
    )
    own_flat = own_columns * ext_count + own_index[:, None, :]
    own_values = projector[0, 0] * own_zin[:, None, :]
    table_own = (
        jnp.zeros((atom_count * proj_count * ext_count,), jnp.float32)
        .at[own_flat.reshape(-1)]
        .add(own_values.reshape(-1))
    )
    table_own = table_own.reshape(atom_count, proj_count, ext_count)
    return (table_near, table_own)


def apply_hamiltonian(orbital_block, local_potential, tables, coupling_own):
    table_near, table_own = tables
    orb_count = orbital_block.shape[0]
    atom_count, proj_count = coupling_own.shape
    flat_block = orbital_block.reshape(orb_count, -1)
    extended = with_halo(orbital_block, (("gx", 1), ("gy", 2)), 6)
    kinetic = kinetic_part(extended, orbital_block)
    partial_terms = jnp.einsum("ijanc,bc->ijanb", table_near, flat_block, precision=highest)
    received = with_halo(partial_terms.reshape(1, 1, -1), (("gx", 0), ("gy", 1)), 1)
    grouped = received.reshape(3, 3, 3, 3, atom_count, proj_count, orb_count)
    coefficients = grouped[1, 1, 1, 1]
    for row_pos in range(3):
        for col_pos in range(3):
            if row_pos != 1 or col_pos != 1:
                coefficients = coefficients + grouped[row_pos, col_pos, 2 - row_pos, 2 - col_pos]
    scaled = coupling_own[:, :, None] * coefficients
    near_coefs = with_halo(scaled.reshape(1, 1, -1), (("gx", 0), ("gy", 1)), 1)
    near_coefs = near_coefs.reshape(3, 3, atom_count, proj_count, orb_count)
    projector_term = jnp.einsum("ijanc,ijanb->bc", table_near, near_coefs, precision=highest)
    return kinetic + local_potential * orbital_block + projector_term.reshape(orbital_block.shape)


def inverse_factor(intersection):
    factor = jnp.linalg.cholesky(intersection)
    identity = jnp.eye(intersection.shape[0], dtype=jnp.float32)
    return lax.linalg.triangular_solve(factor, identity, left_side=True, lower=True)


def per_device_halo(orbitals, local_potential, atom_cell, support_offset, projector, coupling):
    orb_count, size_x, size_y, size_z = orbitals.shape
    tables = prepare_tables(atom_cell, support_offset, projector, size_x, size_y, size_z)
    coupling_own = coupling[0, 0]

    def hamiltonian(orbital_block):
        return apply_hamiltonian(orbital_block, local_potential, tables, coupling_own)

    middle = 0.5 * (top_edge + low_edge)
    half_width = 0.5 * (top_edge - low_edge)
    total_cells = float(size_x * size_y * size_z * lax.axis_size("gx") * lax.axis_size("gy"))
    band_start = lax.axis_index("band") * orb_count
    first_term = (hamiltonian(orbitals) - middle * orbitals) / half_width
    filtered = 2.0 * (hamiltonian(first_term) - middle * first_term) / half_width - orbitals
    filt_flat = filtered.reshape(orb_count, -1)
    orbs_all = orb_count * lax.axis_size("band")
    empty_square = jnp.zeros((orbs_all, orbs_all), jnp.float32)
    whole_block = lax.all_gather(filt_flat, "band", axis=0, tiled=True)
    over_cols = jnp.einsum("kc,lc->kl", whole_block, filt_flat, precision=highest) / total_cells
    intersection = lax.psum(
        lax.dynamic_update_slice(empty_square, over_cols, (0, band_start)), ("gx", "gy", "band")
    )
    inverse = inverse_factor(intersection)
    rotated_all = jnp.dot(inverse, whole_block, precision=highest)
    rotated = lax.dynamic_slice_in_dim(rotated_all, band_start, orb_count, 0)
    image_own = hamiltonian(rotated.reshape(orbitals.shape)).reshape(orb_count, -1)
    sub_cols = jnp.einsum("kc,lc->kl", rotated_all, image_own, precision=highest) / total_cells
    subspace = lax.psum(
        lax.dynamic_update_slice(empty_square, sub_cols, (0, band_start)), ("gx", "gy", "band")
    )
    cols_own = lax.dynamic_slice_in_dim(subspace, band_start, orb_count, 1)
    residual = (
        image_own - jnp.einsum("kl,kc->lc", cols_own, rotated_all, precision=highest)
    ) / half_width
    return (rotated.reshape(orbitals.shape), residual.reshape(orbitals.shape), subspace)


MESH = pl.DeviceIdType.MESH
reach = 6
box = 2 * reach + 1
box_y = 16
pad_y = 8
scale = -0.5 / spacing**2


def gather_kernel(
    dims, orb_ref, pot_ref, pack_ref, orb_out, pot_out, pack_out, local_sem, send_sem, recv_sem, *stage_sems
):
    dom_x, dom_y, bands = dims
    count = dom_x * dom_y
    my_x, my_y, my_band = lax.axis_index("gx"), lax.axis_index("gy"), lax.axis_index("band")
    me = my_x * dom_y + my_y
    half = pot_ref.shape[0] // bands
    mine = pl.ds(my_band * half, half)

    barrier = pltpu.get_barrier_semaphore()

    def greet(step, carry):
        peer = lax.rem(me + step, count)
        pl.semaphore_signal(
            barrier, inc=1, device_id={"gx": peer // dom_y, "gy": lax.rem(peer, dom_y)}, device_id_type=MESH
        )
        return carry

    lax.fori_loop(1, count, greet, 0)
    for step in range(1, bands):
        pl.semaphore_signal(
            barrier, inc=1, device_id={"band": lax.rem(my_band + step, bands)}, device_id_type=MESH
        )

    def orb_copy(peer, source):
        return pltpu.make_async_remote_copy(
            src_ref=orb_ref.at[peer],
            dst_ref=orb_out.at[source // dom_y, :, lax.rem(source, dom_y)],
            send_sem=send_sem.at[peer],
            recv_sem=recv_sem.at[source],
            device_id={"gx": peer // dom_y, "gy": lax.rem(peer, dom_y)},
            device_id_type=MESH,
        )

    def stage_copies(stage, axis, peer, source):
        if stage == 0:
            pairs = (
                (pack_ref.at[my_band], pack_out.at[my_x * dom_y + source, my_band]),
                (pot_ref.at[mine], pot_out.at[my_x, mine, source]),
            )
        elif stage == 1:
            block = pack_out.at[pl.ds(source * dom_y, dom_y), my_band]
            strip = pot_out.at[source, mine]
            pairs = ((block, block), (strip, strip))
        else:
            block = pack_out.at[:, source]
            strip = pot_out.at[:, pl.ds(source * half, half)]
            pairs = ((block, block), (strip, strip))
        return [
            pltpu.make_async_remote_copy(
                src_ref=src,
                dst_ref=dst,
                send_sem=stage_sems[2 * stage].at[kind, peer],
                recv_sem=stage_sems[2 * stage + 1].at[kind, source],
                device_id={axis: peer},
                device_id_type=MESH,
            )
            for kind, (src, dst) in enumerate(pairs)
        ]

    def start_stage(stage, axis, place, size):
        for step in range(1, size):
            for copy in stage_copies(stage, axis, lax.rem(place + step, size), place):
                copy.start()

    def end_stage(stage, axis, place, size):
        for step in range(1, size):
            peer = lax.rem(place + step, size)
            for copy in stage_copies(stage, axis, peer, place):
                copy.wait_send()
            for copy in stage_copies(stage, axis, peer, peer):
                copy.wait_recv()

    own = [
        pltpu.make_async_copy(pack_ref.at[my_band], pack_out.at[me, my_band], local_sem.at[0]),
        pltpu.make_async_copy(pot_ref.at[mine], pot_out.at[my_x, mine, my_y], local_sem.at[1]),
        pltpu.make_async_copy(orb_ref.at[me], orb_out.at[my_x, :, my_y], local_sem.at[2]),
    ]
    for copy in own:
        copy.start()
    pl.semaphore_wait(barrier, count - 1 + bands - 1)

    def send(step, carry):
        orb_copy(lax.rem(me + step, count), me).start()
        return carry

    def finish(step, carry):
        peer = lax.rem(me + step, count)
        orb_copy(peer, me).wait_send()
        orb_copy(peer, peer).wait_recv()
        return carry

    early = count // 4
    start_stage(0, "gy", my_y, dom_y)
    lax.fori_loop(1, early, send, 0)
    end_stage(0, "gy", my_y, dom_y)
    own[0].wait()
    own[1].wait()
    start_stage(1, "gx", my_x, dom_x)
    lax.fori_loop(early, count, send, 0)
    end_stage(1, "gx", my_x, dom_x)
    start_stage(2, "band", my_band, bands)
    end_stage(2, "band", my_band, bands)
    lax.fori_loop(1, count, finish, 0)
    own[2].wait()


def compute_kernel(
    dims,
    orb_any,
    pot_any,
    pack_any,
    along_ref,
    filt_any,
    image_any,
    table,
    field,
    out,
    sums,
    coefs,
    orb_ref,
    pot_ref,
    pack_ref,
    small,
    copy_sem,
):
    count, atom_count, proj_count, dom_y, size_x, size_y = dims
    nx, ny, nz = orb_ref.shape
    points = pack_ref.shape[3]
    fetch_pack = pltpu.make_async_copy(pack_any, pack_ref, copy_sem.at[0])
    fetch_small = pltpu.make_async_copy(pack_any.at[:, :, proj_count + 1, pl.ds(0, 128)], small, copy_sem.at[1])
    fetch_pack.start()
    fetch_small.start()
    field[...] = jnp.zeros_like(field)
    inside_field = field.at[pl.ds(reach, nx), pl.ds(pad_y, ny), :]
    fetch_field = pltpu.make_async_copy(orb_any, inside_field, copy_sem.at[2])
    fetch_pot = pltpu.make_async_copy(pot_any, pot_ref, copy_sem.at[3])
    fetch_orb = pltpu.make_async_copy(orb_any, orb_ref, copy_sem.at[4])
    fetch_field.start()
    fetch_pot.start()
    fetch_orb.start()

    def home_of(dom, atom):
        cell = small[dom, atom, proj_count].astype(jnp.int32)
        home_x = dom // dom_y * size_x + cell // (size_y * nz)
        home_y = lax.rem(dom, dom_y) * size_y + lax.rem(cell // nz, size_y) + pad_y - reach
        return home_x, home_y, lax.rem(cell, nz)

    rows = box * box_y
    wide = 16
    lane = lax.broadcasted_iota(jnp.int32, (rows, nz), 1)
    row_xy = lax.broadcasted_iota(jnp.int32, (rows, points), 0)
    row_z = lax.broadcasted_iota(jnp.int32, (wide, points), 0)

    def build(dom, carry):
        for atom in range(atom_count):
            cell = pack_ref[dom, atom, proj_count : proj_count + 1, :].astype(jnp.int32)
            hot_xy = jnp.where(row_xy == lax.shift_right_arithmetic(cell, 4), 1.0, 0.0).astype(jnp.bfloat16)
            hot_z = row_z == (cell & 15)
            values = jnp.concatenate(
                [
                    jnp.where(hot_z, pack_ref[dom, atom, n : n + 1, :], 0.0)
                    for n in range(proj_count)
                ],
                axis=0,
            )
            high = values.astype(jnp.bfloat16)
            low = (values - high.astype(jnp.float32)).astype(jnp.bfloat16)
            both = jnp.concatenate([high, low], axis=0)
            boxes = lax.dot_general(hot_xy, both, (((1,), (1,)), ((), ())), preferred_element_type=jnp.float32)
            boxes = boxes + pltpu.roll(boxes, proj_count * wide, 1)
            at = dom * atom_count + atom
            low_z = home_of(dom, atom)[2] - reach
            for n in range(proj_count):
                kept = jnp.where((lane >= n * wide) & (lane < (n + 1) * wide), boxes, 0.0)
                moved = pltpu.roll(kept, lax.rem(low_z - n * wide + 2 * nz, nz), 1)
                table[at, n] = moved.reshape(box, box_y, nz)
        return carry

    out[...] = jnp.zeros_like(out)
    inner = pl.ds(pad_y, ny)
    fetch_pack.wait()
    fetch_small.wait()
    lax.fori_loop(0, count, build, 0, unroll=4)
    fetch_field.wait()
    fetch_pot.wait()
    fetch_orb.wait()

    def hamiltonian():
        def project(at, carry):
            x0, y0, _ = home_of(at // atom_count, lax.rem(at, atom_count))
            totals = [jnp.zeros((box_y, nz), jnp.float32) for _ in range(proj_count)]
            for dx in range(box):
                part = field[x0 + dx, pl.ds(y0, box_y), :]
                for n in range(proj_count):
                    totals[n] = totals[n] + table[at, n, dx] * part
            stacked = [jnp.sum(total, axis=0, keepdims=True) for total in totals]
            sums[at] = jnp.concatenate(stacked, axis=0)
            return carry

        lax.fori_loop(0, count * atom_count, project, 0, unroll=4)
        scaled = jnp.sum(sums[...], axis=2, keepdims=True)
        coefs[...] = jnp.broadcast_to(scaled, coefs.shape)

        chunk = 8
        for start in range(0, nx, chunk):
            block = field[reach + start : reach + start + chunk, pad_y : pad_y + ny, :]
            z_part = jnp.dot(
                block.reshape(chunk * ny, nz), along_ref[...], precision=highest, preferred_element_type=jnp.float32
            )
            out[reach + start : reach + start + chunk, pad_y : pad_y + ny, :] = z_part.reshape(chunk, ny, nz)

        def stencil_row(row, carry):
            at = row + reach
            summed = out[at, inner, :] + pot_ref[row] * field[at, inner, :]
            for k in range(1, reach + 1):
                around = (
                    field[at + k, inner, :]
                    + field[at - k, inner, :]
                    + field[at, pl.ds(pad_y + k, ny), :]
                    + field[at, pl.ds(pad_y - k, ny), :]
                )
                summed = summed + (scale * stencil[k]) * around
            out[at, inner, :] = summed
            return carry

        lax.fori_loop(0, nx, stencil_row, 0, unroll=4)

        def spread(at, carry):
            x0, y0, _ = home_of(at // atom_count, lax.rem(at, atom_count))
            weights = [
                jnp.broadcast_to(
                    coefs[at, n : n + 1, :] * small[at // atom_count, lax.rem(at, atom_count), n], (box_y, nz)
                )
                for n in range(proj_count)
            ]
            for dx in range(box):
                added = out[x0 + dx, pl.ds(y0, box_y), :]
                for n in range(proj_count):
                    added = added + table[at, n, dx] * weights[n]
                out[x0 + dx, pl.ds(y0, box_y), :] = added
            return carry

        lax.fori_loop(0, count * atom_count, spread, 0, unroll=2)

    middle = 0.5 * (top_edge + low_edge)
    half_width = 0.5 * (top_edge - low_edge)
    hamiltonian()

    def first_row(row, carry):
        at = row + reach
        field[at, inner, :] = (out[at, inner, :] - middle * field[at, inner, :]) * (1.0 / half_width)
        return carry

    lax.fori_loop(0, nx, first_row, 0, unroll=4)
    hamiltonian()

    def filter_row(row, carry):
        at = row + reach
        value = (out[at, inner, :] - middle * field[at, inner, :]) * (2.0 / half_width) - orb_ref[row]
        field[at, inner, :] = value
        orb_ref[row] = value
        return carry

    lax.fori_loop(0, nx, filter_row, 0, unroll=4)
    store_filt = pltpu.make_async_copy(orb_ref, filt_any, copy_sem.at[5])
    store_filt.start()
    hamiltonian()
    store_image = pltpu.make_async_copy(out.at[pl.ds(reach, nx), pl.ds(pad_y, ny), :], image_any, copy_sem.at[6])
    store_image.start()
    store_filt.wait()
    store_image.wait()


def project_kernel(
    dims,
    filt_ref,
    image_ref,
    new_out,
    res_out,
    sub_out,
    cells,
    result,
    plane,
    column,
    local_sem,
    send_sem,
    recv_sem,
    plane_send,
    plane_recv,
    column_send,
    column_recv,
    out_sem,
    pair_send,
    pair_recv,
):
    dom_x, dom_y, bands, total_cells = dims
    per_band = dom_x * dom_y
    orbs = per_band * bands
    my_x, my_y, my_band = lax.axis_index("gx"), lax.axis_index("gy"), lax.axis_index("band")
    me = my_band * per_band + my_x * dom_y + my_y
    rows = cells.shape[1] * cells.shape[2]

    def place(peer):
        inside = lax.rem(peer, per_band)
        return {"gx": inside // dom_y, "gy": lax.rem(inside, dom_y), "band": peer // per_band}

    barrier = pltpu.get_barrier_semaphore()

    def greet(step, carry):
        pl.semaphore_signal(barrier, inc=1, device_id=place(lax.rem(me + step, orbs)), device_id_type=MESH)
        return carry

    lax.fori_loop(1, orbs, greet, 0)

    def chunk_of(ref, peer):
        inside = lax.rem(peer, per_band)
        return ref.at[inside // dom_y, peer // per_band, :, lax.rem(inside, dom_y)]

    def parts(peer, source):
        return [
            pltpu.make_async_remote_copy(
                src_ref=chunk_of(ref, peer),
                dst_ref=cells.at[kind * orbs + source],
                send_sem=send_sem.at[kind, peer],
                recv_sem=recv_sem.at[kind, source],
                device_id=place(peer),
                device_id_type=MESH,
            )
            for kind, ref in enumerate((filt_ref, image_ref))
        ]

    own = [
        pltpu.make_async_copy(chunk_of(ref, me), cells.at[kind * orbs + me], local_sem.at[kind])
        for kind, ref in enumerate((filt_ref, image_ref))
    ]
    for copy in own:
        copy.start()
    pl.semaphore_wait(barrier, orbs - 1)

    for kind in range(2):

        def send(step, carry, kind=kind):
            parts(lax.rem(me + step, orbs), me)[kind].start()
            return carry

        lax.fori_loop(1, orbs, send, 0)

    def finish(kind):
        def one(step, carry):
            peer = lax.rem(me + step, orbs)
            parts(peer, me)[kind].wait_send()
            parts(peer, peer)[kind].wait_recv()
            return carry

        lax.fori_loop(1, orbs, one, 0)
        own[kind].wait()

    flat = cells.reshape(2 * orbs * rows, cells.shape[3])
    flat_result = result.reshape(2 * orbs * rows, cells.shape[3])

    def product(left, right, dims_in):
        return lax.dot_general(left, right, (dims_in, ((), ())), precision=highest, preferred_element_type=jnp.float32)

    def load(ref, kind, row):
        return ref[pl.ds(kind * orbs * rows + row, orbs, stride=rows), :]

    in_plane = dom_x * bands
    my_plane = my_x * bands + my_band

    def plane_copy(peer, slot):
        return pltpu.make_async_remote_copy(
            src_ref=plane.at[my_plane],
            dst_ref=plane.at[slot],
            send_sem=plane_send.at[peer],
            recv_sem=plane_recv.at[slot],
            device_id={"gx": peer // bands, "gy": my_y, "band": lax.rem(peer, bands)},
            device_id_type=MESH,
        )

    def column_copy(peer, slot):
        return pltpu.make_async_remote_copy(
            src_ref=column.at[my_y],
            dst_ref=column.at[slot],
            send_sem=column_send.at[peer],
            recv_sem=column_recv.at[slot],
            device_id={"gx": my_x, "gy": peer, "band": my_band},
            device_id_type=MESH,
        )

    def summed(share, box_ref, copy_of, place_at, size):
        box_ref[place_at] = share
        for step in range(1, size):
            copy_of(lax.rem(place_at + step, size), place_at).start()
        for step in range(1, size):
            peer = lax.rem(place_at + step, size)
            copy_of(peer, place_at).wait_send()
            copy_of(peer, peer).wait_recv()
        total = box_ref[0]
        for slot in range(1, size):
            total = total + box_ref[slot]
        return total

    def all_sum(share):
        share = summed(share, plane, plane_copy, my_plane, in_plane)
        return summed(share, column, column_copy, my_y, dom_y) * (1.0 / total_cells)

    sums_across = plane.shape[1] // 2
    groups = orbs // sums_across

    def dense(square):
        return jnp.concatenate([square[g * sums_across : (g + 1) * sums_across] for g in range(groups)], axis=1)

    def square_of(packed):
        return jnp.concatenate([packed[:, g * orbs : (g + 1) * orbs] for g in range(groups)], axis=0)

    finish(0)
    gram = jnp.zeros((orbs, orbs), jnp.float32)
    for row in range(rows):
        part = load(flat, 0, row)
        gram = gram + product(part, part, ((1,), (1,)))
    finish(1)
    mixed_gram = jnp.zeros((orbs, orbs), jnp.float32)
    for row in range(rows):
        mixed_gram = mixed_gram + product(load(flat, 0, row), load(flat, 1, row), ((1,), (1,)))
    totals = all_sum(jnp.concatenate([dense(gram), dense(mixed_gram)], axis=0))
    total = square_of(totals[:sums_across])
    crossed = square_of(totals[sums_across:])

    row_at = lax.broadcasted_iota(jnp.int32, (orbs, orbs), 0)
    col_at = lax.broadcasted_iota(jnp.int32, (orbs, orbs), 1)
    eye = jnp.where(row_at == col_at, 1.0, 0.0)
    work = jnp.concatenate([total, eye], axis=1)
    row_wide = lax.broadcasted_iota(jnp.int32, (orbs, 2 * orbs), 0)
    for k in range(orbs):
        pivot_row = work[k : k + 1, :]
        pivot = work[k : k + 1, k : k + 1]
        factor = jnp.where(row_wide[:, :1] > k, work[:, k : k + 1] / pivot, 0.0)
        work = work - factor * pivot_row
    diagonal = jnp.sum(work[:, :orbs] * eye, axis=1, keepdims=True)
    inverse = work[:, orbs:] / jnp.sqrt(diagonal)

    outs = (new_out, res_out)

    def pair_copy(kind, other, half):
        return pltpu.make_async_remote_copy(
            src_ref=result.at[pl.ds(kind * orbs + other * per_band, per_band)],
            dst_ref=outs[kind].at[:, half],
            send_sem=pair_send.at[kind, other],
            recv_sem=pair_recv.at[kind, half],
            device_id={"gx": my_x, "gy": my_y, "band": other},
            device_id_type=MESH,
        )

    def keep(kind):
        source = result.at[pl.ds(kind * orbs + my_band * per_band, per_band)]
        return pltpu.make_async_copy(source, outs[kind].at[:, my_band], out_sem.at[kind])

    def give(kind):
        for step in range(1, bands):
            pair_copy(kind, lax.rem(my_band + step, bands), my_band).start()
        keep(kind).start()

    for row in range(rows):
        flat_result[pl.ds(row, orbs, stride=rows), :] = product(inverse, load(flat, 0, row), ((1,), (0,)))
    give(0)

    projected = product(inverse, crossed, ((1,), (0,)))
    subspace = product(projected, inverse, ((1,), (1,)))
    sub_out[...] = subspace
    half_width = 0.5 * (top_edge - low_edge)
    mixed = product(subspace, inverse, ((0,), (0,))) * (-1.0 / half_width)
    rotation = jnp.concatenate([mixed, inverse * (1.0 / half_width)], axis=1)
    for row in range(rows):
        both = jnp.concatenate([load(flat, 0, row), load(flat, 1, row)], axis=0)
        flat_result[pl.ds(orbs * rows + row, orbs, stride=rows), :] = product(rotation, both, ((1,), (0,)))
    give(1)

    for kind in range(2):
        for step in range(1, bands):
            other = lax.rem(my_band + step, bands)
            pair_copy(kind, other, my_band).wait_send()
            pair_copy(kind, other, other).wait_recv()
        keep(kind).wait()


def per_device_whole(orbitals, local_potential, atom_cell, support_offset, projector, coupling):
    orb_count, size_x, size_y, nz = orbitals.shape
    dom_x, dom_y, bands = lax.axis_size("gx"), lax.axis_size("gy"), lax.axis_size("band")
    count = dom_x * dom_y
    nx, ny = dom_x * size_x, dom_y * size_y
    atom_count, proj_count, points = projector.shape[2:]
    atoms = count * atom_count
    any_spec = pl.BlockSpec(memory_space=pl.ANY)
    vmem = pl.BlockSpec(memory_space=pltpu.VMEM)

    cell = atom_cell[0, 0]
    offset = support_offset[:, 0, 0]
    home_z = cell % nz
    point_z = home_z[:, None] + offset[2]
    box_cell = ((offset[0] + reach) * box_y + offset[1] + reach) * 16 + offset[2] + reach
    box_cell = jnp.where((point_z >= 0) & (point_z < nz), box_cell, -1).astype(jnp.float32)
    small = jnp.concatenate([coupling[0, 0], cell[:, None].astype(jnp.float32)], axis=1)
    pack = jnp.concatenate(
        [
            projector[0, 0],
            box_cell[:, None],
            jnp.pad(small, ((0, 0), (0, points - small.shape[1])))[:, None],
            jnp.zeros((atom_count, 8 - proj_count - 2, points), jnp.float32),
        ],
        axis=1,
    )
    f32 = jnp.float32
    whole_orb, whole_pot, packs = pl.pallas_call(
        functools.partial(gather_kernel, (dom_x, dom_y, bands)),
        out_shape=(
            jax.ShapeDtypeStruct((dom_x, size_x, dom_y, size_y, nz), f32),
            jax.ShapeDtypeStruct((dom_x, size_x, dom_y, size_y, nz), f32),
            jax.ShapeDtypeStruct((count, atom_count, 8, points), f32),
        ),
        in_specs=[any_spec] * 3,
        out_specs=(any_spec,) * 3,
        scratch_shapes=[
            pltpu.SemaphoreType.DMA((3,)),
            pltpu.SemaphoreType.DMA((count,)),
            pltpu.SemaphoreType.DMA((count,)),
        ]
        + [pltpu.SemaphoreType.DMA((2, size)) for size in (dom_y, dom_x, bands) for _ in range(2)],
        compiler_params=pltpu.CompilerParams(collective_id=0, has_side_effects=True),
    )(orbitals, local_potential, pack)

    along = np.zeros((nz, nz), np.float32)
    for i in range(nz):
        for j in range(max(0, i - reach), min(nz, i + reach + 1)):
            along[i, j] = scale * stencil[abs(i - j)] * (3.0 if i == j else 1.0)

    field_shape = (nx + 2 * reach, ny + 2 * pad_y + 8, nz)
    filt, image = pl.pallas_call(
        functools.partial(compute_kernel, (count, atom_count, proj_count, dom_y, size_x, size_y)),
        out_shape=(jax.ShapeDtypeStruct((nx, ny, nz), f32),) * 2,
        in_specs=[any_spec] * 3 + [vmem],
        out_specs=(any_spec, any_spec),
        scratch_shapes=[
            pltpu.VMEM((atoms, proj_count, box, box_y, nz), f32),
            pltpu.VMEM(field_shape, f32),
            pltpu.VMEM(field_shape, f32),
            pltpu.VMEM((atoms, proj_count, nz), f32),
            pltpu.VMEM((atoms, proj_count, nz), f32),
            pltpu.VMEM((nx, ny, nz), f32),
            pltpu.VMEM((nx, ny, nz), f32),
            pltpu.VMEM(packs.shape, f32),
            pltpu.SMEM((count, atom_count, 128), f32),
            pltpu.SemaphoreType.DMA((7,)),
        ],
        compiler_params=pltpu.CompilerParams(vmem_limit_bytes=48 << 20),
    )(whole_orb.reshape(nx, ny, nz), whole_pot.reshape(nx, ny, nz), packs, jnp.asarray(along))

    orbs = orb_count * bands
    sum_rows = orbs // max(1, nz // orbs)
    half = size_x // bands
    rows = half * size_y
    shape = (dom_x, bands, half, dom_y, size_y, nz)
    sem = pltpu.SemaphoreType.DMA
    new, res, sub = pl.pallas_call(
        functools.partial(project_kernel, (dom_x, dom_y, bands, float(nx * ny * nz))),
        out_shape=(
            jax.ShapeDtypeStruct((orb_count, bands, half, size_y, nz), f32),
            jax.ShapeDtypeStruct((orb_count, bands, half, size_y, nz), f32),
            jax.ShapeDtypeStruct((orbs, orbs), f32),
        ),
        in_specs=[any_spec] * 2,
        out_specs=(any_spec, any_spec, vmem),
        scratch_shapes=[
            pltpu.VMEM((2 * orbs, half, size_y, nz), f32),
            pltpu.VMEM((2 * orbs, half, size_y, nz), f32),
            pltpu.VMEM((dom_x * bands, 2 * sum_rows, orbs * orbs // sum_rows), f32),
            pltpu.VMEM((dom_y, 2 * sum_rows, orbs * orbs // sum_rows), f32),
            sem((2,)),
            sem((2, orbs)),
            sem((2, orbs)),
            sem((dom_x * bands,)),
            sem((dom_x * bands,)),
            sem((dom_y,)),
            sem((dom_y,)),
            sem((2,)),
            sem((2, bands)),
            sem((2, bands)),
        ],
        compiler_params=pltpu.CompilerParams(
            collective_id=1, has_side_effects=True, vmem_limit_bytes=32 << 20
        ),
    )(filt.reshape(shape), image.reshape(shape))
    return (new.reshape(orbitals.shape), res.reshape(orbitals.shape), sub)


def per_device(orbitals, local_potential, atom_cell, support_offset, projector, coupling):
    domains = lax.axis_size("gx") * lax.axis_size("gy")
    bands = lax.axis_size("band")
    if orbitals.shape[0] == domains and orbitals.shape[1] % bands == 0 and atom_cell.shape[2] == bands:
        plan = per_device_whole
    else:
        plan = per_device_halo
    return plan(orbitals, local_potential, atom_cell, support_offset, projector, coupling)


def solution(mesh):
    in_specs = (
        P("band", "gx", "gy", None),
        P("gx", "gy", None),
        P("gx", "gy", None),
        P(None, "gx", "gy", None, None),
        P("gx", "gy", None, None, None),
        P("gx", "gy", None, None),
    )
    out_specs = (P("band", "gx", "gy", None), P("band", "gx", "gy", None), P())
    return jax.shard_map(
        per_device, mesh=mesh, in_specs=in_specs, out_specs=out_specs, check_vma=False
    )
```
